128 devices in a mesh: rep: 4 (over y), seq: 32 (over x, z, core).
Axes of the slice: x: 4, y: 4, z: 4, core: 2. Of those that a mesh axis runs over, the one named last changes fastest.
Arguments:
- query: bfloat16 [20480, 4096], P(('rep', 'seq')), parts along dimension 0, may hold values from -320 to 320
- key: bfloat16 [20480, 4096], P(('rep', 'seq')), parts along dimension 0, may hold values from -6 to 6
- value: bfloat16 [20480, 4096], P(('rep', 'seq')), parts along dimension 0, may hold values from -6 to 6
- latent: bfloat16 [16, 128, 640], P('rep', 'seq'), parts along dimension 0, may hold values from -6 to 6
- band_rows: int32 [128], P('rep'), parts along dimension 0, may hold values from 2 to 6, as said below
- head_weight: bfloat16 [4096, 64], replicated, may hold values from -1.1953125 to 1.1953125
- conv_in: bfloat16 [3, 3, 3, 16, 384], replicated, may hold values from -0.3125 to 0.3125
- conv_mid: bfloat16 [3, 3, 3, 384, 384], replicated, may hold values from -0.0625 to 0.0625
- gamma: float32 [384], replicated, may hold values from 0.25 to 1.75
Outputs:
- frames_out: bfloat16 [16, 192, 40, 384], P('rep', 'seq'), parts along dimension 0
The draws below stay inside these ranges and needn't reach their ends.
There are 4 independent parts, one for each index of `rep`. The reference program is written for one: setup_inputs(seed, part) draws one part's arguments, and reference() takes and returns one part's arrays. A program takes and returns all parts, laid end to end along the dimension named above; an argument that names none is the same for every part. Nothing has to cross between parts.
Inputs may be any that keep to these rules, and one draw needn't show every extreme that they name: `band_rows`: devices come in pairs 2p, 2p+1 whose counts are 4 + s and 4 - s with s from 0 to 2; some pair has s = 2.
All inputs are finite; a program needn't handle non-finite values.
Results may differ from the reference program's by a relative error of at most 0.018.
Values may be sent and summed in bfloat16 or wider, within the bound.
A program may use at most 64 MiB of HBM per device.

```python
import math
import jax
import jax.numpy as jnp
from jax import lax

HEADS = 32
HEAD = 128
LAT_CH = 16
CH = 384
FRAMES = 4
BAND = 2
PCOLS = 20
LCOLS = 40
TOKENS = 5120
ROWS = 128
MOST = 6
N_SEQ = 32


def shared_keys(key, strength):
    key_norm = jax.random.fold_in(key, 0)
    key_spot = jax.random.fold_in(key, 2)
    key_pick = jax.random.fold_in(key, 3)
    normal_draw = jnp.clip(jax.random.normal(key_norm, (TOKENS, HEADS * HEAD), jnp.float32), -6.0, 6.0)
    key_rows = normal_draw
    targets = 2 * jax.random.randint(key_spot, (8,), 0, TOKENS // 2)
    query_rows = jnp.arange(8) * (TOKENS // 8) + jax.random.randint(key_pick, (8,), 0, TOKENS // 8)
    levels = jnp.array([12.0, 18.0, 25.0, 12.0, 18.0, 25.0, 15.0, 21.0], jnp.float32)
    shrink = 1.0 - strength * 0.177 / levels
    key_rows = key_rows.at[targets + 1].set(key_rows[targets] * shrink[:, None])
    return (key_rows, targets, query_rows, levels * strength)


def draw_key(key, part):
    key_rows, targets, query_rows, factors = shared_keys(key, 0.0)
    return key_rows.astype(jnp.bfloat16)


def draw_query(key, part):
    key_rows, targets, query_rows, factors = shared_keys(key, 0.0)
    own_part = 2.0 * jnp.clip(jax.random.normal(jax.random.fold_in(key, 5), (TOKENS, HEADS * HEAD), jnp.float32), -6.0, 6.0)
    own_part = own_part.at[query_rows].add(key_rows[targets] * factors[:, None])
    return own_part.astype(jnp.bfloat16)


def draw_band_rows(key, part):
    key = jax.random.fold_in(key, 11)
    key_size, key_wide = jax.random.split(key)
    surplus = jax.random.randint(key_size, (N_SEQ // 2,), 0, BAND + 1)
    widest = jax.random.randint(key_wide, (), 0, N_SEQ // 2)
    surplus = jnp.where(jnp.arange(N_SEQ // 2) == widest, BAND, surplus)
    pairs = jnp.stack([2 * BAND + surplus, 2 * BAND - surplus], axis=1)
    return pairs.reshape(N_SEQ).astype(jnp.int32)


def block_levels(rng, shape, shards, smallest, largest):
    def one(dim, blocks):
        steps = jax.random.uniform(jax.random.fold_in(jax.random.fold_in(rng, 6), dim), (blocks,), jnp.float32, smallest / len(shards), largest / len(shards))
        return jnp.repeat(jnp.exp(steps), shape[dim] // blocks).reshape((-1,) + (1,) * (len(shape) - dim - 1))

    level = one(*shards[0])
    for cut in shards[1:]:
        level = level * one(*cut)
    return level


def gaussian(rng, dims, scale, reach, cuts=(), kind=jnp.bfloat16):
    values = jax.random.normal(rng, dims, jnp.float32) * scale
    if len(cuts) > 0:
        values = block_levels(rng, dims, cuts, -0.22, 0.18) * values
    return jnp.clip(values, min=-reach, max=reach).astype(kind)


def setup_inputs(seed: int = 0, part: int = 0) -> dict:
    key_of = jax.random.split(jax.random.key(seed), 10)
    part_keys = jax.random.split(jax.random.fold_in(key_of[9], part), 10)
    return {
        "query": draw_query(jax.random.fold_in(jax.random.fold_in(key_of[9], part), 71), part),
        "key": draw_key(jax.random.fold_in(jax.random.fold_in(key_of[9], part), 71), part),
        "value": gaussian(part_keys[2], (TOKENS, HEADS * HEAD), 1.0, 6.0, ((0, 32),)),
        "latent": gaussian(part_keys[3], (FRAMES, ROWS, LCOLS * LAT_CH), 1.0, 6.0, ((1, 32),)),
        "band_rows": draw_band_rows(jax.random.fold_in(jax.random.fold_in(key_of[9], part), 71), part),
        "head_weight": gaussian(key_of[5], (HEADS * HEAD, 4 * LAT_CH), 0.2, 1.1953125),
        "conv_in": gaussian(key_of[6], (3, 3, 3, LAT_CH, CH), (27 * LAT_CH) ** -0.5, 0.3125),
        "conv_mid": gaussian(key_of[7], (3, 3, 3, CH, CH), (27 * CH) ** -0.5, 0.0625),
        "gamma": jnp.clip(1.0 + 0.15 * jax.random.normal(key_of[8], (CH,), jnp.float32), 0.25, 1.75),
    }


def causal_conv(field, weight):
    padded = jnp.pad(field, ((2, 0), (1, 1), (1, 1), (0, 0)))
    return lax.conv_general_dilated(padded[None], weight, (1, 1, 1), 'VALID', dimension_numbers=('NDHWC', 'DHWIO', 'NDHWC'), preferred_element_type=jnp.float32)[0]

def reference(query, key, value, latent, band_rows, head_weight, conv_in, conv_mid, gamma):
    score_scale = 1.0 / math.sqrt(HEAD)
    q_heads = query.reshape(TOKENS, HEADS, HEAD).transpose(1, 0, 2)
    k_heads = key.reshape(TOKENS, HEADS, HEAD).transpose(1, 0, 2)
    v_heads = value.reshape(TOKENS, HEADS, HEAD).transpose(1, 0, 2)

    def one_head(triple):
        q_part, k_part, v_part = triple
        scores = jnp.dot(q_part, k_part.T, preferred_element_type=jnp.float32) * score_scale
        peaks = lax.optimization_barrier(jnp.max(scores, axis=1, keepdims=True))
        weights = jnp.exp(scores - peaks)
        totals = lax.optimization_barrier(jnp.sum(weights, axis=1, keepdims=True))
        result = jnp.dot(weights.astype(jnp.bfloat16), v_part, preferred_element_type=jnp.float32) / totals
        return result.astype(jnp.bfloat16)
    attended = lax.map(one_head, (q_heads, k_heads, v_heads))
    attended = attended.transpose(1, 0, 2).reshape(TOKENS, HEADS * HEAD)
    velocity = jnp.dot(attended, head_weight, preferred_element_type=jnp.float32)
    grid = velocity.reshape(N_SEQ, FRAMES, BAND, PCOLS, 2, 2, LAT_CH).transpose(1, 0, 2, 4, 3, 5, 6)
    grid = grid.reshape(FRAMES, ROWS, LCOLS * LAT_CH)
    clean = (latent.astype(jnp.float32) - 0.9 * grid).astype(jnp.bfloat16)
    field = clean.reshape(FRAMES, ROWS, LCOLS, LAT_CH)
    first_conv = causal_conv(field, conv_in).astype(jnp.bfloat16)
    values32 = first_conv.astype(jnp.float32)
    normed = values32 * lax.rsqrt(lax.optimization_barrier(jnp.mean(values32 * values32, axis=-1, keepdims=True)) + 1e-06) * gamma
    normed = jax.nn.silu(normed).astype(jnp.bfloat16)
    decoded = (values32 + causal_conv(normed, conv_mid)).astype(jnp.bfloat16)
    row_start = (jnp.cumsum(band_rows) - band_rows).astype(jnp.int32)
    slot_ids = jnp.arange(MOST, dtype=jnp.int32)
    row_ids = row_start[:, None] + slot_ids[None, :]
    keep_mask = (slot_ids[None, :] < band_rows[:, None]).reshape(-1)
    row_ids = jnp.clip(row_ids, 0, ROWS - 1).reshape(-1).astype(jnp.int32)
    picked = jnp.take(decoded, row_ids, axis=1)
    return jnp.where(keep_mask[None, :, None, None], picked, jnp.zeros_like(picked))
```

```python
import functools
import math

import jax
import jax.numpy as jnp
from jax import lax
from jax.experimental import pallas as pl
from jax.experimental.pallas import tpu as pltpu
from jax.sharding import PartitionSpec as P

HEADS = 32
HEAD = 128
LAT_CH = 16
FRAMES = 4
BAND = 2
PCOLS = 20
TOK = 160
TOKENS = 5120
SEQ = 32
QB = 640
KB = 1280
NQ = TOKENS // QB
NK = TOKENS // KB
SCALE = math.log2(math.e) / math.sqrt(HEAD)
NEG = -1e30

CHIPS = (
    (0, 0), (1, 0), (3, 0), (0, 1), (0, 3), (1, 1), (3, 3), (1, 3),
    (3, 1), (2, 0), (0, 2), (2, 1), (1, 2), (2, 3), (3, 2), (2, 2),
)
ARRIVE = ("K0", "Q0", "Q1", "Q2", "Q3", "K1", "Q4", "Q5", "K2", "K3", "Q6", "Q7")


def plan_tiles():
    keys, queries, tiles = [], [], []
    for name in ARRIVE:
        place = int(name[1])
        if name[0] == "K":
            fresh = [(q, place) for q in queries]
            keys.append(place)
        else:
            fresh = [(place, k) for k in keys]
            queries.append(place)
        tiles += fresh
    seen_q, seen_k, rows = set(), set(), []
    for t, (q, k) in enumerate(tiles):
        last = all(u[0] != q for u in tiles[t + 1:])
        rows.append((q, k, int(q not in seen_q), int(k not in seen_k), int(last)))
        seen_q.add(q)
        seen_k.add(k)
    return rows


TILES = plan_tiles()


def packed_table(values, bits):
    per = 24 // bits
    words = []
    for at in range(0, len(values), per):
        word = 0
        for i, value in enumerate(values[at:at + per]):
            word |= value << (bits * i)
        words.append(word)

    def look(index):
        word = jnp.int32(words[0])
        for i in range(1, len(words)):
            word = jnp.where(index >= i * per, jnp.int32(words[i]), word)
        shift = lax.rem(index, per) * bits
        return lax.shift_right_logical(word, shift) & ((1 << bits) - 1)

    return look


def attend_kernel(
    q_hbm, k_hbm, v_hbm, w_ref, out_ref,
    v_in, v_send, q_got, k_got, v_got, q2, k2, v2, acc_ref, top_ref, s_ref, tile_top,
    y_send, y_got, in_sem, q_ssem, k_ssem, v_ssem, q_rsem, k_rsem, v_rsem, y_ssem, y_rsem,
):
    me = lax.axis_index("seq")
    my_x, my_z, my_c = me // 8, lax.rem(me // 2, 4), lax.rem(me, 2)
    look_dx = packed_table([c[0] for c in CHIPS], 2)
    look_dz = packed_table([c[1] for c in CHIPS], 2)

    def ahead(j):
        chip = j // 2
        x = lax.rem(my_x + look_dx(chip), 4)
        z = lax.rem(my_z + look_dz(chip), 4)
        return x * 8 + z * 2 + lax.rem(my_c + j, 2)

    def behind(j):
        chip = j // 2
        x = lax.rem(my_x + 4 - look_dx(chip), 4)
        z = lax.rem(my_z + 4 - look_dz(chip), 4)
        return x * 8 + z * 2 + lax.rem(my_c + j, 2)

    def head_cols(h):
        return pl.ds(pl.multiple_of(h * HEAD, HEAD), HEAD)

    def slot_rows(j):
        return pl.ds(pl.multiple_of(j * TOK, 32), TOK)

    def q_copy(j):
        to = ahead(j)
        return pltpu.make_async_remote_copy(
            src_ref=q_hbm.at[:, head_cols(to)], dst_ref=q_got.at[slot_rows(j)],
            send_sem=q_ssem.at[j], recv_sem=q_rsem.at[j],
            device_id={"seq": to}, device_id_type=pl.DeviceIdType.MESH,
        )

    def k_copy(j):
        to = ahead(j)
        return pltpu.make_async_remote_copy(
            src_ref=k_hbm.at[:, head_cols(to)], dst_ref=k_got.at[slot_rows(j)],
            send_sem=k_ssem.at[j], recv_sem=k_rsem.at[j],
            device_id={"seq": to}, device_id_type=pl.DeviceIdType.MESH,
        )

    def v_copy(j):
        return pltpu.make_async_remote_copy(
            src_ref=v_send.at[j], dst_ref=v_got.at[j],
            send_sem=v_ssem.at[j], recv_sem=v_rsem.at[j],
            device_id={"seq": ahead(j)}, device_id_type=pl.DeviceIdType.MESH,
        )

    def y_copy(j):
        return pltpu.make_async_remote_copy(
            src_ref=y_send.at[j], dst_ref=y_got.at[j],
            send_sem=y_ssem.at[j], recv_sem=y_rsem.at[j],
            device_id={"seq": behind(j)}, device_id_type=pl.DeviceIdType.MESH,
        )

    v_load = pltpu.make_async_copy(v_hbm, v_in, in_sem.at[0])
    q_own = pltpu.make_async_copy(q_hbm.at[:, head_cols(me)], q_got.at[pl.ds(0, TOK)], in_sem.at[1])
    k_own = pltpu.make_async_copy(k_hbm.at[:, head_cols(me)], k_got.at[pl.ds(0, TOK)], in_sem.at[2])
    v_load.start()
    q_own.start()
    k_own.start()
    barrier = pltpu.get_barrier_semaphore()

    def greet(j, carry):
        pl.semaphore_signal(
            barrier, inc=1, device_id={"seq": ahead(j)}, device_id_type=pl.DeviceIdType.MESH
        )
        return carry

    lax.fori_loop(1, SEQ, greet, 0)
    v_load.wait()

    def project(j):
        h = ahead(j)
        values = v_in[:, head_cols(h)]
        y = jnp.dot(values, w_ref[head_cols(h), :], preferred_element_type=jnp.float32)
        return jnp.concatenate([y[:80], y[80:]], axis=1).astype(jnp.bfloat16)

    def project_step(j, carry):
        v_send[j] = project(j)
        return carry

    lax.fori_loop(0, SEQ, project_step, 0, unroll=4)
    pl.semaphore_wait(barrier, SEQ - 1)

    def send_k(j, carry):
        k_copy(j).start()
        v_copy(j).start()
        return carry

    def send_q(j, carry):
        q_copy(j).start()
        return carry

    for name in ARRIVE:
        place = int(name[1])
        if name[0] == "K":
            lax.fori_loop(max(1, place * 8), place * 8 + 8, send_k, 0)
        else:
            lax.fori_loop(max(1, place * 4), place * 4 + 4, send_q, 0)

    def q_rows(i):
        return pl.ds(pl.multiple_of(i * QB, QB), QB)

    def k_rows(i):
        return pl.ds(pl.multiple_of(i * KB, KB), KB)

    def prep_q(i):
        def one(u, carry):
            j = i * 4 + u

            @pl.when(j == 0)
            def _():
                q_own.wait()

            @pl.when(j > 0)
            def _():
                q_copy(j).wait_recv()

            return carry

        lax.fori_loop(0, 4, one, 0)
        rows = q_rows(i)
        scaled = q_got[rows, :].astype(jnp.float32) * SCALE
        high = scaled.astype(jnp.bfloat16)
        q2[rows, :HEAD] = high
        q2[rows, HEAD:] = (scaled - high.astype(jnp.float32)).astype(jnp.bfloat16)
        acc_ref[rows, :] = jnp.zeros((QB, HEAD), jnp.float32)
        top_ref[rows, :] = jnp.full((QB, HEAD), NEG, jnp.float32)

    def prep_k(i):
        lane = lax.broadcasted_iota(jnp.int32, (80, HEAD), 1)
        ones = jnp.where(lane == 64, 1.0, 0.0)

        def one(u, carry):
            j = i * 8 + u

            @pl.when(j == 0)
            def _():
                k_own.wait()
                v_got[0] = v_send[0]

            @pl.when(j > 0)
            def _():
                k_copy(j).wait_recv()
                v_copy(j).wait_recv()

            both = v_got[j].astype(jnp.float32)
            left = jnp.where(lane < 64, both, ones)
            right = jnp.where(lane < 64, pltpu.roll(both, 64, 1), ones)
            at = pl.multiple_of(j * TOK, 32)
            v2[pl.ds(at, 80), :] = left.astype(jnp.bfloat16)
            v2[pl.ds(at + 80, 80), :] = right.astype(jnp.bfloat16)
            return carry

        lax.fori_loop(0, 8, one, 0)
        rows = k_rows(i)
        k2[rows, :HEAD] = k_got[rows, :]
        k2[rows, HEAD:] = k_got[rows, :]

    def finish(i):
        rows = q_rows(i)
        total = acc_ref[rows, :]
        y = total * (1.0 / total[:, 64:65])
        for u in range(4):
            j = i * 4 + u
            part = y[u * TOK:(u + 1) * TOK]
            merged = jnp.where(
                lax.broadcasted_iota(jnp.int32, (80, HEAD), 1) < 64,
                part[:80], pltpu.roll(part[80:], 64, 1),
            )
            y_send[j] = merged.astype(jnp.bfloat16)

        def one(u, carry):
            j = i * 4 + u

            @pl.when(j > 0)
            def _():
                y_copy(j).start()

            return carry

        lax.fori_loop(0, 4, one, 0)

    look_q = packed_table([t[0] for t in TILES], 3)
    look_k = packed_table([t[1] for t in TILES], 2)
    look_new_q = packed_table([t[2] for t in TILES], 1)
    look_new_k = packed_table([t[3] for t in TILES], 1)
    look_last = packed_table([t[4] for t in TILES], 1)

    def ready(t):
        @pl.when(look_new_k(t) == 1)
        def _():
            prep_k(look_k(t))

        @pl.when(look_new_q(t) == 1)
        def _():
            prep_q(look_q(t))

    def score(t, slot):
        s = lax.dot_general(
            q2[q_rows(look_q(t)), :], k2[k_rows(look_k(t)), :],
            (((1,), (1,)), ((), ())), preferred_element_type=jnp.float32,
        )
        s_ref[slot] = s
        top = s[:, :HEAD]
        for u in range(1, KB // HEAD):
            top = jnp.maximum(top, s[:, u * HEAD:(u + 1) * HEAD])
        tile_top[slot] = top

    def weigh(t, slot):
        rows = q_rows(look_q(t))
        before = top_ref[rows, :]
        now = jnp.maximum(before, jnp.max(tile_top[slot], axis=1, keepdims=True))
        top_ref[rows, :] = now
        weights = jnp.exp2(s_ref[slot] - jnp.concatenate([now] * (KB // HEAD), axis=1))
        acc_ref[rows, :] = acc_ref[rows, :] * jnp.exp2(before - now) + jnp.dot(
            weights.astype(jnp.bfloat16), v2[k_rows(look_k(t)), :],
            preferred_element_type=jnp.float32,
        )

    def after(t):
        @pl.when(look_last(t) == 1)
        def _():
            finish(look_q(t))

    def step(t, slot):
        ready(t + 1)
        score(t + 1, 1 - slot)
        weigh(t, slot)
        after(t)

    def two_steps(i, carry):
        step(2 * i, 0)
        step(2 * i + 1, 1)
        return carry

    count = len(TILES)
    ready(jnp.int32(0))
    score(jnp.int32(0), 0)
    lax.fori_loop(0, (count - 2) // 2, two_steps, 0)
    step(jnp.int32(count - 2), 0)
    weigh(jnp.int32(count - 1), 1)
    after(jnp.int32(count - 1))

    def gather(j, total):
        y_copy(j).wait_recv()
        return total + y_got[j].astype(jnp.float32)

    out_ref[...] = lax.fori_loop(1, SEQ, gather, y_send[0].astype(jnp.float32))

    def drain(j, carry):
        q_copy(j).wait_send()
        k_copy(j).wait_send()
        v_copy(j).wait_send()
        y_copy(j).wait_send()
        return carry

    lax.fori_loop(1, SEQ, drain, 0)


def attend(query, key, value, head_weight):
    bf16, f32 = jnp.bfloat16, jnp.float32
    any_space = pl.BlockSpec(memory_space=pl.ANY)
    vmem = pl.BlockSpec(memory_space=pltpu.VMEM)
    return pl.pallas_call(
        attend_kernel,
        out_shape=jax.ShapeDtypeStruct((80, HEAD), f32),
        in_specs=[any_space, any_space, any_space, vmem],
        out_specs=vmem,
        scratch_shapes=[
            pltpu.VMEM((TOK, HEADS * HEAD), bf16),
            pltpu.VMEM((SEQ, 80, HEAD), bf16),
            pltpu.VMEM((TOKENS, HEAD), bf16),
            pltpu.VMEM((TOKENS, HEAD), bf16),
            pltpu.VMEM((SEQ, 80, HEAD), bf16),
            pltpu.VMEM((TOKENS, 2 * HEAD), bf16),
            pltpu.VMEM((TOKENS, 2 * HEAD), bf16),
            pltpu.VMEM((TOKENS, HEAD), bf16),
            pltpu.VMEM((TOKENS, HEAD), f32),
            pltpu.VMEM((TOKENS, HEAD), f32),
            pltpu.VMEM((2, QB, KB), f32),
            pltpu.VMEM((2, QB, HEAD), f32),
            pltpu.VMEM((SEQ, 80, HEAD), bf16),
            pltpu.VMEM((SEQ, 80, HEAD), bf16),
            pltpu.SemaphoreType.DMA((3,)),
        ] + [pltpu.SemaphoreType.DMA((SEQ,))] * 8,
        compiler_params=pltpu.CompilerParams(
            collective_id=1, has_side_effects=True, vmem_limit_bytes=56 * 2**20
        ),
        cost_estimate=pl.CostEstimate(
            flops=4 * TOKENS * TOKENS * HEAD, bytes_accessed=16 * 2**20,
            transcendentals=TOKENS * TOKENS,
        ),
        name="attend",
    )(query, key, value, head_weight)


def with_halo(cells, width):
    count = lax.axis_size("seq")
    ends = count - 1
    head = cells[:, :width]
    tail = cells[:, cells.shape[1] - width:]
    return jnp.concatenate(
        [
            lax.ppermute(tail, "seq", [(i, i + 1) for i in range(ends)]),
            cells,
            lax.ppermute(head, "seq", [(i + 1, i) for i in range(ends)]),
        ],
        axis=1,
    )


def causal_conv(field, weight):
    padded = jnp.pad(field, ((2, 0), (0, 0), (1, 1), (0, 0)))
    return lax.conv_general_dilated(
        padded[None],
        weight,
        (1, 1, 1),
        "VALID",
        dimension_numbers=("NDHWC", "DHWIO", "NDHWC"),
        preferred_element_type=jnp.float32,
    )[0]


def decode_rows(window, first_row, total_rows, conv_in, conv_mid, gamma):
    first_conv = causal_conv(window, conv_in).astype(jnp.bfloat16)
    values32 = first_conv.astype(jnp.float32)
    row_ids = first_row + 1 + jnp.arange(first_conv.shape[1], dtype=jnp.int32)
    inside = (row_ids >= 0) & (row_ids < total_rows)
    normed = (
        values32 * lax.rsqrt(jnp.mean(values32 * values32, axis=-1, keepdims=True) + 1e-06) * gamma
    )
    normed = jnp.where(inside[None, :, None, None], jax.nn.silu(normed), 0.0).astype(jnp.bfloat16)
    mid_conv = causal_conv(normed, conv_mid)
    return (values32[:, 1:-1] + mid_conv).astype(jnp.bfloat16)


def per_device(query, key, value, latent, band_rows, head_weight, conv_in, conv_mid, gamma):
    place = lax.axis_index("seq")
    groups = lax.axis_size("seq")
    packed = attend(query, key, value, head_weight)
    velocity = jnp.concatenate([packed[:, :64], packed[:, 64:]], axis=0)
    band_len = 2 * BAND
    lat_cols = latent.shape[2] // LAT_CH
    grid = velocity.reshape(FRAMES, BAND, PCOLS, 2, 2, LAT_CH).transpose(0, 1, 3, 2, 4, 5)
    grid = grid.reshape(FRAMES, band_len, lat_cols * LAT_CH)
    clean = (latent.astype(jnp.float32) - 0.9 * grid).astype(jnp.bfloat16)
    window = with_halo(clean, 2)
    decoded = decode_rows(
        window.reshape(FRAMES, band_len + 4, lat_cols, LAT_CH),
        place * band_len - 2,
        band_len * groups,
        conv_in,
        conv_mid,
        gamma,
    )
    length = jnp.sum(jnp.where(jnp.arange(groups, dtype=jnp.int32) == place, band_rows, 0))
    extra = lax.ppermute(decoded[:, :BAND], "seq", [(i + 1, i) for i in range(0, groups, 2)])
    lead = jnp.where(lax.rem(place, 2) == 1, band_len - length, 0)
    extended = jnp.concatenate([decoded, extra, jnp.zeros_like(extra)], axis=1)
    picked = lax.dynamic_slice_in_dim(extended, lead, 3 * BAND, 1)
    keep_mask = jnp.arange(3 * BAND, dtype=jnp.int32) < length
    return jnp.where(keep_mask[None, :, None, None], picked, jnp.zeros_like(picked))


def solution(mesh):
    return jax.shard_map(
        per_device,
        mesh=mesh,
        in_specs=(
            P(("rep", "seq"), None),
            P(("rep", "seq"), None),
            P(("rep", "seq"), None),
            P("rep", "seq", None),
            P("rep"),
            P(),
            P(),
            P(),
            P(),
        ),
        out_specs=P("rep", "seq", None, None),
        check_vma=False,
    )
```

```python
import functools
import math

import jax
import jax.numpy as jnp
from jax import lax
from jax.experimental import pallas as pl
from jax.experimental.pallas import tpu as pltpu
from jax.sharding import PartitionSpec as P

HEADS = 32
HEAD = 128
LAT_CH = 16
CH = 384
FRAMES = 4
BAND = 2
PCOLS = 20
LCOLS = 40
TOK = 160
TOKENS = 5120
SEQ = 32
QB = 640
KB = 1280
NQ = TOKENS // QB
NK = TOKENS // KB
SCALE = math.log2(math.e) / math.sqrt(HEAD)
NEG = -1e30
V_AFTER = 1

CHIPS = (
    (0, 0), (1, 0), (3, 0), (0, 1), (0, 3), (1, 1), (3, 3), (1, 3),
    (3, 1), (2, 0), (0, 2), (2, 1), (1, 2), (2, 3), (3, 2), (2, 2),
)
ARRIVE = ("K0", "Q0", "Q1", "Q2", "Q3", "K1", "Q4", "Q5", "K2", "K3", "Q6", "Q7")


def plan_tiles():
    keys, queries, tiles = [], [], []
    for name in ARRIVE:
        place = int(name[1])
        if name[0] == "K":
            fresh = [(q, place) for q in queries]
            keys.append(place)
        else:
            fresh = [(place, k) for k in keys]
            queries.append(place)
        tiles += fresh
    seen_q, seen_k, rows = set(), set(), []
    for t, (q, k) in enumerate(tiles):
        last = all(u[0] != q for u in tiles[t + 1:])
        rows.append((q, k, int(q not in seen_q), int(k not in seen_k), int(last)))
        seen_q.add(q)
        seen_k.add(k)
    return rows


TILES = plan_tiles()


def packed_table(values, bits):
    per = 24 // bits
    words = []
    for at in range(0, len(values), per):
        word = 0
        for i, value in enumerate(values[at:at + per]):
            word |= value << (bits * i)
        words.append(word)

    def look(index):
        word = jnp.int32(words[0])
        for i in range(1, len(words)):
            word = jnp.where(index >= i * per, jnp.int32(words[i]), word)
        shift = lax.rem(index, per) * bits
        return lax.shift_right_logical(word, shift) & ((1 << bits) - 1)

    return look


def attend_kernel(
    q_hbm, k_hbm, v_hbm, w_hbm, out_ref,
    v_in, w_in, v_send, q_got, k_got, v_got, q2, k2, v2, acc_ref, top_ref, s_ref, tile_top,
    y_send, y_got, in_sem, send_sem, q_sem, k_sem, v_sem, y_sem,
):
    me = lax.axis_index("seq")
    my_x, my_z, my_c = me // 8, lax.rem(me // 2, 4), lax.rem(me, 2)
    look_dx = packed_table([c[0] for c in CHIPS], 2)
    look_dz = packed_table([c[1] for c in CHIPS], 2)

    def ahead(j):
        chip = j // 2
        x = lax.rem(my_x + look_dx(chip), 4)
        z = lax.rem(my_z + look_dz(chip), 4)
        return x * 8 + z * 2 + lax.rem(my_c + j, 2)

    def behind(j):
        chip = j // 2
        x = lax.rem(my_x + 4 - look_dx(chip), 4)
        z = lax.rem(my_z + 4 - look_dz(chip), 4)
        return x * 8 + z * 2 + lax.rem(my_c + j, 2)

    def head_cols(h):
        return pl.ds(pl.multiple_of(h * HEAD, HEAD), HEAD)

    def slot_rows(j):
        return pl.ds(pl.multiple_of(j * TOK, 32), TOK)

    def push(source, target, to, which, sem):
        pltpu.make_async_remote_copy(
            src_ref=source, dst_ref=target, send_sem=send_sem.at[which], recv_sem=sem,
            device_id={"seq": to}, device_id_type=pl.DeviceIdType.MESH,
        ).start()

    def arrived(ref, sem):
        pltpu.make_async_copy(ref, ref, sem).wait()

    v_load = pltpu.make_async_copy(v_hbm, v_in, in_sem.at[0])
    w_load = pltpu.make_async_copy(w_hbm, w_in, in_sem.at[1])
    v_load.start()
    w_load.start()
    pltpu.make_async_copy(k_hbm.at[:, head_cols(me)], k_got.at[pl.ds(0, TOK)], k_sem.at[0]).start()
    pltpu.make_async_copy(q_hbm.at[:, head_cols(me)], q_got.at[pl.ds(0, TOK)], q_sem.at[0]).start()
    barrier = pltpu.get_barrier_semaphore()

    def greet(j, carry):
        pl.semaphore_signal(
            barrier, inc=1, device_id={"seq": ahead(j)}, device_id_type=pl.DeviceIdType.MESH
        )
        return carry

    lax.fori_loop(1, SEQ, greet, 0)
    pl.semaphore_wait(barrier, SEQ - 1)

    def send_k(j, carry):
        to = ahead(j)
        push(k_hbm.at[:, head_cols(to)], k_got.at[slot_rows(j)], to, 0, k_sem.at[j // 8])
        return carry

    def send_q(j, carry):
        to = ahead(j)
        push(q_hbm.at[:, head_cols(to)], q_got.at[slot_rows(j)], to, 1, q_sem.at[j // 4])
        return carry

    def send_v(j, carry):
        push(v_send.at[j], v_got.at[j], ahead(j), 2, v_sem.at[j // 8])
        return carry

    def project(j, carry):
        h = ahead(j)
        y = lax.dot_general(
            v_in[:, head_cols(h)], w_in[:, head_cols(h)],
            (((1,), (1,)), ((), ())), preferred_element_type=jnp.float32,
        )
        v_send[j] = jnp.concatenate([y[:80], y[80:]], axis=1).astype(jnp.bfloat16)
        return carry

    pending = []
    for at, name in enumerate(ARRIVE):
        place = int(name[1])
        if name[0] == "K":
            lax.fori_loop(max(1, place * 8), place * 8 + 8, send_k, 0)
            pending.append(place)
        else:
            lax.fori_loop(max(1, place * 4), place * 4 + 4, send_q, 0)
        if at >= V_AFTER and pending:
            if pending[0] == 0:
                v_load.wait()
                w_load.wait()
            for chunk in pending:
                lax.fori_loop(chunk * 8, chunk * 8 + 8, project, 0, unroll=4)
                lax.fori_loop(max(1, chunk * 8), chunk * 8 + 8, send_v, 0)
            if pending[0] == 0:
                pltpu.make_async_copy(v_send.at[0], v_got.at[0], v_sem.at[0]).start()
            pending = []

    def q_rows(i):
        return pl.ds(pl.multiple_of(i * QB, QB), QB)

    def k_rows(i):
        return pl.ds(pl.multiple_of(i * KB, KB), KB)

    def prep_q(i):
        rows = q_rows(i)
        arrived(q_got.at[rows], q_sem.at[i])
        scaled = q_got[rows, :].astype(jnp.float32) * SCALE
        high = scaled.astype(jnp.bfloat16)
        q2[rows, :HEAD] = high
        q2[rows, HEAD:] = (scaled - high.astype(jnp.float32)).astype(jnp.bfloat16)
        acc_ref[rows, :] = jnp.zeros((QB, HEAD), jnp.float32)
        top_ref[rows, :] = jnp.full((QB, HEAD), NEG, jnp.float32)

    def prep_k(i):
        lane = lax.broadcasted_iota(jnp.int32, (80, HEAD), 1)
        ones = jnp.where(lane == 64, 1.0, 0.0)
        rows = k_rows(i)
        arrived(k_got.at[rows], k_sem.at[i])
        k2[rows, :HEAD] = k_got[rows, :]
        k2[rows, HEAD:] = k_got[rows, :]
        slots = pl.ds(pl.multiple_of(i * 8, 8), 8)
        arrived(v_got.at[slots], v_sem.at[i])
        for u in range(8):
            j = i * 8 + u
            both = v_got[j].astype(jnp.float32)
            left = jnp.where(lane < 64, both, ones)
            right = jnp.where(lane < 64, pltpu.roll(both, 64, 1), ones)
            at = pl.multiple_of(j * TOK, 32)
            v2[pl.ds(at, 80), :] = left.astype(jnp.bfloat16)
            v2[pl.ds(at + 80, 80), :] = right.astype(jnp.bfloat16)

    def finish(i):
        rows = q_rows(i)
        total = acc_ref[rows, :]
        y = total * (1.0 / total[:, 64:65])
        for u in range(4):
            j = i * 4 + u
            part = y[u * TOK:(u + 1) * TOK]
            merged = jnp.where(
                lax.broadcasted_iota(jnp.int32, (80, HEAD), 1) < 64,
                part[:80], pltpu.roll(part[80:], 64, 1),
            )
            y_send[j] = merged.astype(jnp.bfloat16)

        def one(u, carry):
            j = i * 4 + u

            @pl.when(j > 0)
            def _():
                push(y_send.at[j], y_got.at[j], behind(j), 3, y_sem)

            return carry

        lax.fori_loop(0, 4, one, 0)

    look_q = packed_table([t[0] for t in TILES], 3)
    look_k = packed_table([t[1] for t in TILES], 2)
    look_new_q = packed_table([t[2] for t in TILES], 1)
    look_new_k = packed_table([t[3] for t in TILES], 1)
    look_last = packed_table([t[4] for t in TILES], 1)

    def ready(t):
        @pl.when(look_new_k(t) == 1)
        def _():
            prep_k(look_k(t))

        @pl.when(look_new_q(t) == 1)
        def _():
            prep_q(look_q(t))

    def score(t, slot):
        s = lax.dot_general(
            q2[q_rows(look_q(t)), :], k2[k_rows(look_k(t)), :],
            (((1,), (1,)), ((), ())), preferred_element_type=jnp.float32,
        )
        s_ref[slot] = s
        top = s[:, :HEAD]
        for u in range(1, KB // HEAD):
            top = jnp.maximum(top, s[:, u * HEAD:(u + 1) * HEAD])
        tile_top[slot] = top

    def weigh(t, slot):
        rows = q_rows(look_q(t))
        before = top_ref[rows, :]
        now = jnp.maximum(before, jnp.max(tile_top[slot], axis=1, keepdims=True))
        top_ref[rows, :] = now
        weights = jnp.exp2(s_ref[slot] - jnp.concatenate([now] * (KB // HEAD), axis=1))
        acc_ref[rows, :] = acc_ref[rows, :] * jnp.exp2(before - now) + jnp.dot(
            weights.astype(jnp.bfloat16), v2[k_rows(look_k(t)), :],
            preferred_element_type=jnp.float32,
        )

    def after(t):
        @pl.when(look_last(t) == 1)
        def _():
            finish(look_q(t))

    def step(t, slot):
        ready(t + 1)
        score(t + 1, 1 - slot)
        weigh(t, slot)
        after(t)

    def two_steps(i, carry):
        step(2 * i, 0)
        step(2 * i + 1, 1)
        return carry

    count = len(TILES)
    ready(jnp.int32(0))
    score(jnp.int32(0), 0)
    lax.fori_loop(0, (count - 2) // 2, two_steps, 0)
    step(jnp.int32(count - 2), 0)
    weigh(jnp.int32(count - 1), 1)
    after(jnp.int32(count - 1))

    others = pl.ds(1, SEQ - 1)
    arrived(y_got.at[others], y_sem)

    def gather(j, total):
        return total + y_got[j].astype(jnp.float32)

    out_ref[...] = lax.fori_loop(1, SEQ, gather, y_send[0].astype(jnp.float32), unroll=True)
    arrived(k_got.at[pl.ds(TOK, TOKENS - TOK)], send_sem.at[0])
    arrived(q_got.at[pl.ds(TOK, TOKENS - TOK)], send_sem.at[1])
    arrived(v_got.at[others], send_sem.at[2])
    arrived(y_got.at[others], send_sem.at[3])


def attend(query, key, value, head_weight):
    bf16, f32 = jnp.bfloat16, jnp.float32
    any_space = pl.BlockSpec(memory_space=pl.ANY)
    return pl.pallas_call(
        attend_kernel,
        out_shape=jax.ShapeDtypeStruct((80, HEAD), f32),
        in_specs=[any_space] * 4,
        out_specs=pl.BlockSpec(memory_space=pltpu.VMEM),
        scratch_shapes=[
            pltpu.VMEM((TOK, HEADS * HEAD), bf16),
            pltpu.VMEM((64, HEADS * HEAD), bf16),
            pltpu.VMEM((SEQ, 80, HEAD), bf16),
            pltpu.VMEM((TOKENS, HEAD), bf16),
            pltpu.VMEM((TOKENS, HEAD), bf16),
            pltpu.VMEM((SEQ, 80, HEAD), bf16),
            pltpu.VMEM((TOKENS, 2 * HEAD), bf16),
            pltpu.VMEM((TOKENS, 2 * HEAD), bf16),
            pltpu.VMEM((TOKENS, HEAD), bf16),
            pltpu.VMEM((TOKENS, HEAD), f32),
            pltpu.VMEM((TOKENS, HEAD), f32),
            pltpu.VMEM((2, QB, KB), f32),
            pltpu.VMEM((2, QB, HEAD), f32),
            pltpu.VMEM((SEQ, 80, HEAD), bf16),
            pltpu.VMEM((SEQ, 80, HEAD), bf16),
            pltpu.SemaphoreType.DMA((2,)),
            pltpu.SemaphoreType.DMA((4,)),
            pltpu.SemaphoreType.DMA((NQ,)),
            pltpu.SemaphoreType.DMA((NK,)),
            pltpu.SemaphoreType.DMA((NK,)),
            pltpu.SemaphoreType.DMA,
        ],
        compiler_params=pltpu.CompilerParams(
            collective_id=1, has_side_effects=True, vmem_limit_bytes=56 * 2**20
        ),
        cost_estimate=pl.CostEstimate(
            flops=4 * TOKENS * TOKENS * HEAD, bytes_accessed=16 * 2**20,
            transcendentals=TOKENS * TOKENS,
        ),
        name="attend",
    )(query, key, value, head_weight.T)


def decode_kernel(
    vel_ref, lat_ref, w_first, w_mid, gamma_ref, out_ref,
    turned, win, own, above, below, near, first_in, w1, first, wide, taps, total, w2, extra,
    in_sem, halo_ssem, halo_rsem, pair_sem,
):
    me = lax.axis_index("seq")
    up, down = lax.rem(me + SEQ - 1, SEQ), lax.rem(me + 1, SEQ)
    odd = lax.rem(me, 2)
    bf16, f32 = jnp.bfloat16, jnp.float32
    w_load = pltpu.make_async_copy(w_mid, w2, in_sem.at[0])
    w_load.start()
    barrier = pltpu.get_barrier_semaphore()
    for to in (up, down):
        pl.semaphore_signal(
            barrier, inc=1, device_id={"seq": to}, device_id_type=pl.DeviceIdType.MESH
        )

    lane20 = lax.broadcasted_iota(jnp.int32, (80, HEAD), 1)
    vel = vel_ref[...]
    for o in range(8):
        turn = vel if o == 0 else pltpu.roll(vel, HEAD - LAT_CH * o, 1)
        turned[o] = jnp.where(lane20 < LAT_CH, turn, 0.0)
    win[...] = jnp.zeros_like(win)
    for f in range(FRAMES):
        for r in range(BAND):
            for a in range(2):
                for b in range(2):
                    o = (f // 2) * 4 + a * 2 + b
                    row = f * 8 + 2 + 2 * r + a
                    win[row, pl.ds(8 + b, PCOLS, stride=2), :] = turned[
                        o, pl.ds(((f % 2) * BAND + r) * PCOLS, PCOLS), :
                    ]
    own[:, LCOLS:, :] = jnp.zeros((4, 8, HEAD), f32)
    for y in range(4):
        merged = jnp.zeros((LCOLS, HEAD), f32)
        for f in range(FRAMES):
            grid = win[f * 8 + 2 + y, 8:48, :]
            clean = (lat_ref[f * 4 + y] - 0.9 * grid).astype(bf16).astype(f32)
            win[f * 8 + 2 + y, 8:48, :] = clean
            merged = merged + (clean if f == 0 else pltpu.roll(clean, LAT_CH * f, 1))
        own[y, 0:LCOLS, :] = merged
    near[0] = own[0:2].astype(bf16)
    near[1] = own[2:4].astype(bf16)
    pl.semaphore_wait(barrier, 2)
    to_up = pltpu.make_async_remote_copy(
        src_ref=near.at[0], dst_ref=below, send_sem=halo_ssem.at[0], recv_sem=halo_rsem.at[0],
        device_id={"seq": up}, device_id_type=pl.DeviceIdType.MESH,
    )
    to_down = pltpu.make_async_remote_copy(
        src_ref=near.at[1], dst_ref=above, send_sem=halo_ssem.at[1], recv_sem=halo_rsem.at[1],
        device_id={"seq": down}, device_id_type=pl.DeviceIdType.MESH,
    )
    to_up.start()
    to_down.start()

    w1[...] = jnp.zeros_like(w1)
    for s in range(3):
        w1[s * HEAD:s * HEAD + 48, :] = w_first[s * 3]
        w1[s * HEAD + 64:s * HEAD + 112, :] = w_first[s * 3 + 1]
    w1[384:432, :] = w_first[2]
    w1[448:496, :] = w_first[5]
    w1[512:560, :] = w_first[8]
    wide[:, 0:8, :] = jnp.zeros((FRAMES * 6, 8, CH), f32)
    wide[:, 48:56, :] = jnp.zeros((FRAMES * 6, 8, CH), f32)

    to_up.wait_recv()
    to_down.wait_recv()
    lane40 = lax.broadcasted_iota(jnp.int32, (LCOLS, HEAD), 1)
    for side in range(2):
        there = (me > 0) if side == 0 else (me < SEQ - 1)
        got = above if side == 0 else below
        for y in range(2):
            rows = jnp.where(there, got[y, 0:LCOLS, :].astype(f32), 0.0)
            for f in range(FRAMES):
                part = rows if f == 0 else pltpu.roll(rows, HEAD - LAT_CH * f, 1)
                win[f * 8 + (0 if side == 0 else 6) + y, 8:48, :] = jnp.where(
                    lane40 < LAT_CH, part, 0.0
                )

    def gather_columns(f, carry):
        parts = []
        for y in range(8):
            row = f * 8 + y
            parts.append(
                win[row, 7:47, :]
                + pltpu.roll(win[row, 8:48, :], LAT_CH, 1)
                + pltpu.roll(win[row, 9:49, :], 2 * LAT_CH, 1)
            )
        block = jnp.concatenate(parts, axis=0)
        pair = block[0:240] + pltpu.roll(block[40:280], 64, 1)
        single = block[80:320]
        first_in[f, :, 256:384] = pair.astype(bf16)
        first_in[f, :, 512:640] = single.astype(bf16)
        for later in (1, 2):
            @pl.when(f + later < FRAMES)
            def _():
                first_in[f + later, :, (2 - later) * HEAD:(3 - later) * HEAD] = pair.astype(bf16)

        total[f] = single
        return carry

    lax.fori_loop(0, FRAMES, gather_columns, 0)
    blank = jnp.zeros((240, HEAD), bf16)
    first_in[0, :, 0:128] = blank
    first_in[0, :, 128:256] = blank
    first_in[1, :, 0:128] = blank
    first_in[0, :, 384:512] = blank
    first_in[1, :, 384:512] = pltpu.roll(total[0], 64, 1).astype(bf16)
    first_in[2, :, 384:512] = (total[0] + pltpu.roll(total[1], 64, 1)).astype(bf16)
    first_in[3, :, 384:512] = (total[1] + pltpu.roll(total[2], 64, 1)).astype(bf16)

    def first_step(f, carry):
        conv = jnp.dot(first_in[f], w1[...], preferred_element_type=f32)
        values = conv.astype(bf16).astype(f32)
        power = jnp.mean(values * values, axis=1, keepdims=True)
        normed = values * lax.rsqrt(power + 1e-06) * gamma_ref[...]
        normed = normed / (1.0 + jnp.exp(-normed))
        place = lax.broadcasted_iota(jnp.int32, (240, CH), 0)
        outside = ((place < 40) & (me == 0)) | ((place >= 200) & (me == SEQ - 1))
        normed = jnp.where(outside, 0.0, normed)
        first[f] = values[40:200]
        for y in range(6):
            wide[f * 6 + y, 8:48, :] = normed[y * 40:(y + 1) * 40]
        for u in range(3):
            for w in range(3):
                rows = [wide[f * 6 + y + u, 7 + w:47 + w, :] for y in range(4)]
                at = (u * 3 + w) * CH
                taps[f, :, at:at + CH] = jnp.concatenate(rows, axis=0).astype(bf16)
        return carry

    lax.fori_loop(0, FRAMES, first_step, 0)
    w_load.wait()
    for s in (2, 1, 0):
        count = FRAMES - (2 - s)
        for part in range(3):
            cols = slice(part * 3 * CH, (part + 1) * 3 * CH)
            term = jnp.dot(
                taps[0:count, :, cols].reshape(count * TOK, 3 * CH), w2[s, cols, :],
                preferred_element_type=f32,
            ).reshape(count, TOK, CH)
            first[2 - s:FRAMES] = first[2 - s:FRAMES] + term

    out_ref[:, 0:TOK, :] = first[...].astype(bf16)
    hand = pltpu.make_async_remote_copy(
        src_ref=out_ref.at[:, pl.ds(0, 80), :], dst_ref=extra,
        send_sem=pair_sem.at[0], recv_sem=pair_sem.at[1],
        device_id={"seq": me - odd}, device_id_type=pl.DeviceIdType.MESH,
    )

    @pl.when(odd == 1)
    def _():
        hand.start()
        hand.wait_send()
        out_ref[:, TOK:TOK + 80, :] = jnp.zeros((FRAMES, 80, CH), bf16)

    @pl.when(odd == 0)
    def _():
        hand.wait_recv()
        out_ref[:, TOK:TOK + 80, :] = extra[...]

    to_up.wait_send()
    to_down.wait_send()


def decode(velocity, latent, conv_in, conv_mid, gamma):
    bf16, f32 = jnp.bfloat16, jnp.float32
    vmem = pl.BlockSpec(memory_space=pltpu.VMEM)
    spaced = latent.reshape(FRAMES * 4, LCOLS, LAT_CH).astype(f32)
    spaced = jnp.pad(spaced, ((0, 0), (0, 0), (0, HEAD - LAT_CH)))
    return pl.pallas_call(
        decode_kernel,
        out_shape=jax.ShapeDtypeStruct((FRAMES, TOK + 80, CH), bf16),
        in_specs=[vmem, vmem, vmem, pl.BlockSpec(memory_space=pl.ANY), vmem],
        out_specs=vmem,
        scratch_shapes=[
            pltpu.VMEM((8, 80, HEAD), f32),
            pltpu.VMEM((FRAMES * 8, 56, HEAD), f32),
            pltpu.VMEM((4, 48, HEAD), f32),
            pltpu.VMEM((2, 48, HEAD), bf16),
            pltpu.VMEM((2, 48, HEAD), bf16),
            pltpu.VMEM((2, 2, 48, HEAD), bf16),
            pltpu.VMEM((FRAMES, 240, 640), bf16),
            pltpu.VMEM((640, CH), bf16),
            pltpu.VMEM((FRAMES, TOK, CH), f32),
            pltpu.VMEM((FRAMES * 6, 56, CH), f32),
            pltpu.VMEM((FRAMES, TOK, 9 * CH), bf16),
            pltpu.VMEM((FRAMES, 240, HEAD), f32),
            pltpu.VMEM((3, 9 * CH, CH), bf16),
            pltpu.VMEM((FRAMES, 80, CH), bf16),
            pltpu.SemaphoreType.DMA((1,)),
            pltpu.SemaphoreType.DMA((2,)),
            pltpu.SemaphoreType.DMA((2,)),
            pltpu.SemaphoreType.DMA((2,)),
        ],
        compiler_params=pltpu.CompilerParams(
            collective_id=2, has_side_effects=True, vmem_limit_bytes=48 * 2**20
        ),
        cost_estimate=pl.CostEstimate(
            flops=2 * 640 * 27 * CH * CH, bytes_accessed=10 * 2**20, transcendentals=960 * CH
        ),
        name="decode",
    )(
        velocity, spaced, conv_in.reshape(9, 48, CH), conv_mid.reshape(3, 9 * CH, CH),
        gamma.reshape(1, CH),
    )


def per_device(query, key, value, latent, band_rows, head_weight, conv_in, conv_mid, gamma):
    place = lax.axis_index("seq")
    velocity = attend(query, key, value, head_weight)
    decoded = decode(velocity, latent, conv_in, conv_mid, gamma)
    decoded = decoded.reshape(FRAMES, 3 * BAND, LCOLS, CH)
    groups = lax.axis_size("seq")
    length = jnp.sum(jnp.where(jnp.arange(groups, dtype=jnp.int32) == place, band_rows, 0))
    lead = jnp.where(lax.rem(place, 2) == 1, 2 * BAND - length, 0)
    extended = jnp.pad(decoded, ((0, 0), (0, BAND), (0, 0), (0, 0)))
    picked = lax.dynamic_slice_in_dim(extended, lead, 3 * BAND, 1)
    keep_mask = jnp.arange(3 * BAND, dtype=jnp.int32) < length
    return jnp.where(keep_mask[None, :, None, None], picked, jnp.zeros_like(picked))


def solution(mesh):
    return jax.shard_map(
        per_device,
        mesh=mesh,
        in_specs=(
            P(("rep", "seq"), None),
            P(("rep", "seq"), None),
            P(("rep", "seq"), None),
            P("rep", "seq", None),
            P("rep"),
            P(),
            P(),
            P(),
            P(),
        ),
        out_specs=P("rep", "seq", None, None),
        check_vma=False,
    )
```

```python
import functools
import math

import jax
import jax.numpy as jnp
from jax import lax
from jax.experimental import pallas as pl
from jax.experimental.pallas import tpu as pltpu
from jax.sharding import PartitionSpec as P

HEADS = 32
HEAD = 128
LAT_CH = 16
CH = 384
FRAMES = 4
BAND = 2
PCOLS = 20
LCOLS = 40
TOK = 160
TOKENS = 5120
SEQ = 32
QB = 640
KB = 1280
NQ = TOKENS // QB
NK = TOKENS // KB
SCALE = math.log2(math.e) / math.sqrt(HEAD)
NEG = -1e30
V_AFTER = 1

CHIPS = (
    (0, 0), (1, 1), (3, 3), (2, 2), (1, 3), (3, 1), (2, 0), (0, 2),
    (1, 0), (3, 2), (0, 1), (2, 3), (3, 0), (1, 2), (0, 3), (2, 1),
)
ARRIVE = ("K0", "Q0", "Q1", "Q2", "Q3", "K1", "Q4", "Q5", "K2", "K3", "Q6", "Q7")


def plan_tiles():
    keys, queries, tiles = [], [], []
    for name in ARRIVE:
        place = int(name[1])
        if name[0] == "K":
            fresh = [(q, place) for q in queries]
            keys.append(place)
        else:
            fresh = [(place, k) for k in keys]
            queries.append(place)
        tiles += fresh
    seen_q, seen_k, rows = set(), set(), []
    for t, (q, k) in enumerate(tiles):
        last = all(u[0] != q for u in tiles[t + 1:])
        rows.append((q, k, int(q not in seen_q), int(k not in seen_k), int(last)))
        seen_q.add(q)
        seen_k.add(k)
    return rows


TILES = plan_tiles()


def packed_table(values, bits):
    per = 24 // bits
    words = []
    for at in range(0, len(values), per):
        word = 0
        for i, value in enumerate(values[at:at + per]):
            word |= value << (bits * i)
        words.append(word)

    def look(index):
        word = jnp.int32(words[0])
        for i in range(1, len(words)):
            word = jnp.where(index >= i * per, jnp.int32(words[i]), word)
        shift = lax.rem(index, per) * bits
        return lax.shift_right_logical(word, shift) & ((1 << bits) - 1)

    return look


def clip_kernel(
    q_hbm, k_hbm, v_hbm, w_hbm, lat_hbm, first_hbm, mid_hbm, gamma_ref, band_ref, out_ref,
    v_in, w_in, v_send, q_got, k_got, v_got, q2, k2, v2, acc_ref, top_ref, s_ref, tile_top,
    y_send, y_got, in_sem, send_sem, q_sem, k_sem, v_sem, y_sem,
    lat_in, lat, w_first, turned, win, own, above, below, near, first_in, w1, first, wide, taps,
    total, w2, mine, extra, halo_ssem, halo_rsem, pair_sem,
):
    bf16, f32 = jnp.bfloat16, jnp.float32
    me = lax.axis_index("seq")
    my_x, my_z, my_c = me // 8, lax.rem(me // 2, 4), lax.rem(me, 2)
    look_dx = packed_table([c[0] for c in CHIPS], 2)
    look_dz = packed_table([c[1] for c in CHIPS], 2)

    def ahead(j):
        chip = j // 2
        x = lax.rem(my_x + look_dx(chip), 4)
        z = lax.rem(my_z + look_dz(chip), 4)
        return x * 8 + z * 2 + lax.rem(my_c + j, 2)

    def behind(j):
        chip = j // 2
        x = lax.rem(my_x + 4 - look_dx(chip), 4)
        z = lax.rem(my_z + 4 - look_dz(chip), 4)
        return x * 8 + z * 2 + lax.rem(my_c + j, 2)

    def head_cols(h):
        return pl.ds(pl.multiple_of(h * HEAD, HEAD), HEAD)

    def slot_rows(j):
        return pl.ds(pl.multiple_of(j * TOK, 32), TOK)

    def push(source, target, to, which, sem):
        pltpu.make_async_remote_copy(
            src_ref=source, dst_ref=target, send_sem=send_sem.at[which], recv_sem=sem,
            device_id={"seq": to}, device_id_type=pl.DeviceIdType.MESH,
        ).start()

    def arrived(ref, sem):
        pltpu.make_async_copy(ref, ref, sem).wait()

    v_load = pltpu.make_async_copy(v_hbm, v_in, in_sem.at[0])
    w_load = pltpu.make_async_copy(w_hbm, w_in, in_sem.at[1])
    v_load.start()
    w_load.start()
    pltpu.make_async_copy(k_hbm.at[:, head_cols(me)], k_got.at[pl.ds(0, TOK)], k_sem.at[0]).start()
    pltpu.make_async_copy(q_hbm.at[:, head_cols(me)], q_got.at[pl.ds(0, TOK)], q_sem.at[0]).start()
    barrier = pltpu.get_barrier_semaphore()

    def greet(j, carry):
        pl.semaphore_signal(
            barrier, inc=1, device_id={"seq": ahead(j)}, device_id_type=pl.DeviceIdType.MESH
        )
        return carry

    lax.fori_loop(1, SEQ, greet, 0)
    pl.semaphore_wait(barrier, SEQ - 1)

    def send_k(j, carry):
        to = ahead(j)
        push(k_hbm.at[:, head_cols(to)], k_got.at[slot_rows(j)], to, 0, k_sem.at[j // 8])
        return carry

    def send_q(j, carry):
        to = ahead(j)
        push(q_hbm.at[:, head_cols(to)], q_got.at[slot_rows(j)], to, 1, q_sem.at[j // 4])
        return carry

    def send_v(j, carry):
        push(v_send.at[j], v_got.at[j], ahead(j), 2, v_sem.at[j // 8])
        return carry

    def project(j, carry):
        h = ahead(j)
        y = lax.dot_general(
            v_in[:, head_cols(h)], w_in[:, head_cols(h)],
            (((1,), (1,)), ((), ())), preferred_element_type=jnp.float32,
        )
        v_send[j] = jnp.concatenate([y[:80], y[80:]], axis=1).astype(jnp.bfloat16)
        return carry

    pending = []
    for at, name in enumerate(ARRIVE):
        place = int(name[1])
        if name[0] == "K":
            lax.fori_loop(max(1, place * 8), place * 8 + 8, send_k, 0)
            pending.append(place)
        else:
            lax.fori_loop(max(1, place * 4), place * 4 + 4, send_q, 0)
        if at >= V_AFTER and pending:
            if pending[0] == 0:
                v_load.wait()
                w_load.wait()
            for chunk in pending:
                lax.fori_loop(chunk * 8, chunk * 8 + 8, project, 0, unroll=4)
                lax.fori_loop(max(1, chunk * 8), chunk * 8 + 8, send_v, 0)
            if pending[0] == 0:
                pltpu.make_async_copy(v_send.at[0], v_got.at[0], v_sem.at[0]).start()
            pending = []

    lat_load = pltpu.make_async_copy(lat_hbm, lat_in, in_sem.at[2])
    first_load = pltpu.make_async_copy(first_hbm, w_first, in_sem.at[3])
    mid_load = pltpu.make_async_copy(mid_hbm, w2, in_sem.at[4])
    lat_load.start()
    first_load.start()
    mid_load.start()
    win[...] = jnp.zeros_like(win)
    wide[:, 0:8, :] = jnp.zeros((FRAMES * 6, 8, CH), f32)
    wide[:, 48:56, :] = jnp.zeros((FRAMES * 6, 8, CH), f32)
    own[:, LCOLS:, :] = jnp.zeros((4, 8, HEAD), f32)
    blank = jnp.zeros((240, HEAD), bf16)
    first_in[0, :, 0:128] = blank
    first_in[0, :, 128:256] = blank
    first_in[1, :, 0:128] = blank
    first_in[0, :, 384:512] = blank
    lat_load.wait()
    flat = jnp.concatenate([lat_in[f].astype(f32) for f in range(FRAMES)], axis=0)
    for block in range(5):
        lanes = flat[:, block * HEAD:(block + 1) * HEAD]
        for u in range(8):
            x = block * 8 + u
            lat[x * 16:(x + 1) * 16, :] = lanes if u == 0 else pltpu.roll(lanes, HEAD - LAT_CH * u, 1)
    w1[...] = jnp.zeros_like(w1)
    first_load.wait()
    for s in range(3):
        w1[s * HEAD:s * HEAD + 48, :] = w_first[s * 3]
        w1[s * HEAD + 64:s * HEAD + 112, :] = w_first[s * 3 + 1]
    w1[384:432, :] = w_first[2]
    w1[448:496, :] = w_first[5]
    w1[512:560, :] = w_first[8]

    def q_rows(i):
        return pl.ds(pl.multiple_of(i * QB, QB), QB)

    def k_rows(i):
        return pl.ds(pl.multiple_of(i * KB, KB), KB)

    def prep_q(i):
        rows = q_rows(i)
        arrived(q_got.at[rows], q_sem.at[i])
        scaled = q_got[rows, :].astype(jnp.float32) * SCALE
        high = scaled.astype(jnp.bfloat16)
        q2[rows, :HEAD] = high
        q2[rows, HEAD:] = (scaled - high.astype(jnp.float32)).astype(jnp.bfloat16)
        acc_ref[rows, :] = jnp.zeros((QB, HEAD), jnp.float32)
        top_ref[rows, :] = jnp.full((QB, HEAD), NEG, jnp.float32)

    def prep_k(i):
        lane = lax.broadcasted_iota(jnp.int32, (80, HEAD), 1)
        ones = jnp.where(lane == 64, 1.0, 0.0)
        rows = k_rows(i)
        arrived(k_got.at[rows], k_sem.at[i])
        k2[rows, :HEAD] = k_got[rows, :]
        k2[rows, HEAD:] = k_got[rows, :]
        slots = pl.ds(pl.multiple_of(i * 8, 8), 8)
        arrived(v_got.at[slots], v_sem.at[i])
        for u in range(8):
            j = i * 8 + u
            both = v_got[j].astype(jnp.float32)
            left = jnp.where(lane < 64, both, ones)
            right = jnp.where(lane < 64, pltpu.roll(both, 64, 1), ones)
            at = pl.multiple_of(j * TOK, 32)
            v2[pl.ds(at, 80), :] = left.astype(jnp.bfloat16)
            v2[pl.ds(at + 80, 80), :] = right.astype(jnp.bfloat16)

    def finish(i):
        rows = q_rows(i)
        total = acc_ref[rows, :]
        y = total * (1.0 / total[:, 64:65])
        for u in range(4):
            j = i * 4 + u
            part = y[u * TOK:(u + 1) * TOK]
            merged = jnp.where(
                lax.broadcasted_iota(jnp.int32, (80, HEAD), 1) < 64,
                part[:80], pltpu.roll(part[80:], 64, 1),
            )
            y_send[j] = merged.astype(jnp.bfloat16)

        def one(u, carry):
            j = i * 4 + u

            @pl.when(j > 0)
            def _():
                push(y_send.at[j], y_got.at[j], behind(j), 3, y_sem)

            return carry

        lax.fori_loop(0, 4, one, 0)

    look_q = packed_table([t[0] for t in TILES], 3)
    look_k = packed_table([t[1] for t in TILES], 2)
    look_new_q = packed_table([t[2] for t in TILES], 1)
    look_new_k = packed_table([t[3] for t in TILES], 1)
    look_last = packed_table([t[4] for t in TILES], 1)

    def ready(t):
        @pl.when(look_new_k(t) == 1)
        def _():
            prep_k(look_k(t))

        @pl.when(look_new_q(t) == 1)
        def _():
            prep_q(look_q(t))

    def score(t, slot):
        s = lax.dot_general(
            q2[q_rows(look_q(t)), :], k2[k_rows(look_k(t)), :],
            (((1,), (1,)), ((), ())), preferred_element_type=jnp.float32,
        )
        s_ref[slot] = s
        top = s[:, :HEAD]
        for u in range(1, KB // HEAD):
            top = jnp.maximum(top, s[:, u * HEAD:(u + 1) * HEAD])
        tile_top[slot] = top

    def weigh(t, slot):
        rows = q_rows(look_q(t))
        before = top_ref[rows, :]
        now = jnp.maximum(before, jnp.max(tile_top[slot], axis=1, keepdims=True))
        top_ref[rows, :] = now
        weights = jnp.exp2(s_ref[slot] - jnp.concatenate([now] * (KB // HEAD), axis=1))
        acc_ref[rows, :] = acc_ref[rows, :] * jnp.exp2(before - now) + jnp.dot(
            weights.astype(jnp.bfloat16), v2[k_rows(look_k(t)), :],
            preferred_element_type=jnp.float32,
        )

    def after(t):
        @pl.when(look_last(t) == 1)
        def _():
            finish(look_q(t))

    def step(t, slot):
        ready(t + 1)
        score(t + 1, 1 - slot)
        weigh(t, slot)
        after(t)

    def two_steps(i, carry):
        step(2 * i, 0)
        step(2 * i + 1, 1)
        return carry

    count = len(TILES)
    ready(jnp.int32(0))
    score(jnp.int32(0), 0)
    lax.fori_loop(0, (count - 2) // 2, two_steps, 0)
    step(jnp.int32(count - 2), 0)
    weigh(jnp.int32(count - 1), 1)
    after(jnp.int32(count - 1))

    others = pl.ds(1, SEQ - 1)
    arrived(y_got.at[others], y_sem)

    def gather(j, total):
        return total + y_got[j].astype(jnp.float32)

    vel = lax.fori_loop(1, SEQ, gather, y_send[0].astype(f32), unroll=True)
    up, down = lax.rem(me + SEQ - 1, SEQ), lax.rem(me + 1, SEQ)
    odd = lax.rem(me, 2)
    lane40 = lax.broadcasted_iota(jnp.int32, (LCOLS, HEAD), 1)
    lane20 = lax.broadcasted_iota(jnp.int32, (80, HEAD), 1)
    for o in range(8):
        turn = vel if o == 0 else pltpu.roll(vel, HEAD - LAT_CH * o, 1)
        turned[o] = jnp.where(lane20 < LAT_CH, turn, 0.0)
    for f in range(FRAMES):
        for r in range(BAND):
            for a in range(2):
                for b in range(2):
                    o = (f // 2) * 4 + a * 2 + b
                    row = f * 8 + 2 + 2 * r + a
                    win[row, pl.ds(8 + b, PCOLS, stride=2), :] = turned[
                        o, pl.ds(((f % 2) * BAND + r) * PCOLS, PCOLS), :
                    ]
    for y in range(4):
        merged = jnp.zeros((LCOLS, HEAD), f32)
        for f in range(FRAMES):
            grid = win[f * 8 + 2 + y, 8:48, :]
            clean = (lat[pl.ds(f * 4 + y, LCOLS, stride=16), :] - 0.9 * grid).astype(bf16).astype(f32)
            clean = jnp.where(lane40 < LAT_CH, clean, 0.0)
            win[f * 8 + 2 + y, 8:48, :] = clean
            merged = merged + (clean if f == 0 else pltpu.roll(clean, LAT_CH * f, 1))
        own[y, 0:LCOLS, :] = merged
    near[0] = own[0:2].astype(bf16)
    near[1] = own[2:4].astype(bf16)
    to_up = pltpu.make_async_remote_copy(
        src_ref=near.at[0], dst_ref=below, send_sem=halo_ssem.at[0], recv_sem=halo_rsem.at[0],
        device_id={"seq": up}, device_id_type=pl.DeviceIdType.MESH,
    )
    to_down = pltpu.make_async_remote_copy(
        src_ref=near.at[1], dst_ref=above, send_sem=halo_ssem.at[1], recv_sem=halo_rsem.at[1],
        device_id={"seq": down}, device_id_type=pl.DeviceIdType.MESH,
    )
    to_up.start()
    to_down.start()

    to_up.wait_recv()
    to_down.wait_recv()
    for side in range(2):
        there = (me > 0) if side == 0 else (me < SEQ - 1)
        got = above if side == 0 else below
        for y in range(2):
            rows = jnp.where(there, got[y, 0:LCOLS, :].astype(f32), 0.0)
            for f in range(FRAMES):
                part = rows if f == 0 else pltpu.roll(rows, HEAD - LAT_CH * f, 1)
                win[f * 8 + (0 if side == 0 else 6) + y, 8:48, :] = jnp.where(
                    lane40 < LAT_CH, part, 0.0
                )

    def gather_columns(f, carry):
        parts = []
        for y in range(8):
            row = f * 8 + y
            parts.append(
                win[row, 7:47, :]
                + pltpu.roll(win[row, 8:48, :], LAT_CH, 1)
                + pltpu.roll(win[row, 9:49, :], 2 * LAT_CH, 1)
            )
        block = jnp.concatenate(parts, axis=0)
        pair = block[0:240] + pltpu.roll(block[40:280], 64, 1)
        single = block[80:320]
        first_in[f, :, 256:384] = pair.astype(bf16)
        first_in[f, :, 512:640] = single.astype(bf16)
        for later in (1, 2):
            @pl.when(f + later < FRAMES)
            def _():
                first_in[f + later, :, (2 - later) * HEAD:(3 - later) * HEAD] = pair.astype(bf16)

        total[f] = single
        return carry

    lax.fori_loop(0, FRAMES, gather_columns, 0)
    first_in[1, :, 384:512] = pltpu.roll(total[0], 64, 1).astype(bf16)
    first_in[2, :, 384:512] = (total[0] + pltpu.roll(total[1], 64, 1)).astype(bf16)
    first_in[3, :, 384:512] = (total[1] + pltpu.roll(total[2], 64, 1)).astype(bf16)

    def first_step(f, carry):
        conv = jnp.dot(first_in[f], w1[...], preferred_element_type=f32)
        values = conv.astype(bf16).astype(f32)
        power = jnp.mean(values * values, axis=1, keepdims=True)
        normed = values * lax.rsqrt(power + 1e-06) * gamma_ref[...]
        normed = normed / (1.0 + jnp.exp(-normed))
        place = lax.broadcasted_iota(jnp.int32, (240, CH), 0)
        outside = ((place < 40) & (me == 0)) | ((place >= 200) & (me == SEQ - 1))
        normed = jnp.where(outside, 0.0, normed)
        first[f] = values[40:200]
        for y in range(6):
            wide[f * 6 + y, 8:48, :] = normed[y * 40:(y + 1) * 40]
        for u in range(3):
            for w in range(3):
                rows = [wide[f * 6 + y + u, 7 + w:47 + w, :] for y in range(4)]
                at = (u * 3 + w) * CH
                taps[f, :, at:at + CH] = jnp.concatenate(rows, axis=0).astype(bf16)
        return carry

    lax.fori_loop(0, FRAMES, first_step, 0)
    mid_load.wait()
    for s in (2, 1, 0):
        count = FRAMES - (2 - s)
        for part in range(3):
            cols = slice(part * 3 * CH, (part + 1) * 3 * CH)
            term = jnp.dot(
                taps[0:count, :, cols].reshape(count * TOK, 3 * CH), w2[s, cols, :],
                preferred_element_type=f32,
            ).reshape(count, TOK, CH)
            first[2 - s:FRAMES] = first[2 - s:FRAMES] + term

    mine[...] = first[...].astype(bf16)
    hand = pltpu.make_async_remote_copy(
        src_ref=mine.at[:, pl.ds(0, 80), :], dst_ref=extra,
        send_sem=pair_sem.at[0], recv_sem=pair_sem.at[1],
        device_id={"seq": me - odd}, device_id_type=pl.DeviceIdType.MESH,
    )

    @pl.when(odd == 1)
    def _():
        hand.start()

    length = band_ref[me]
    lead = odd * (2 * BAND - length)
    for f in range(FRAMES):
        for i in range(4):
            row = first[f, i * LCOLS:(i + 1) * LCOLS, :]
            for later in (1, 2):
                if i + later < 4:
                    at = (i + later) * LCOLS
                    row = jnp.where(lead == later, first[f, at:at + LCOLS, :], row)
            row = jnp.where(i < length, row, 0.0)
            out_ref[f, i * LCOLS:(i + 1) * LCOLS, :] = row.astype(bf16)

    @pl.when(odd == 1)
    def _():
        hand.wait_send()
        out_ref[:, TOK:TOK + 80, :] = jnp.zeros((FRAMES, 80, CH), bf16)

    @pl.when(odd == 0)
    def _():
        hand.wait_recv()
        for f in range(FRAMES):
            got = extra[f].astype(f32)
            place = lax.broadcasted_iota(jnp.int32, (80, CH), 0)
            got = jnp.where(place < (length - 4) * LCOLS, got, 0.0)
            out_ref[f, TOK:TOK + 80, :] = got.astype(bf16)

    to_up.wait_send()
    to_down.wait_send()
    arrived(k_got.at[pl.ds(TOK, TOKENS - TOK)], send_sem.at[0])
    arrived(q_got.at[pl.ds(TOK, TOKENS - TOK)], send_sem.at[1])
    arrived(v_got.at[others], send_sem.at[2])
    arrived(y_got.at[others], send_sem.at[3])


def decode_clip(query, key, value, latent, band_rows, head_weight, conv_in, conv_mid, gamma):
    bf16, f32 = jnp.bfloat16, jnp.float32
    any_space = pl.BlockSpec(memory_space=pl.ANY)
    vmem = pl.BlockSpec(memory_space=pltpu.VMEM)
    return pl.pallas_call(
        clip_kernel,
        out_shape=jax.ShapeDtypeStruct((FRAMES, TOK + 80, CH), bf16),
        in_specs=[any_space] * 7 + [vmem, pl.BlockSpec(memory_space=pltpu.SMEM)],
        out_specs=vmem,
        scratch_shapes=[
            pltpu.VMEM((TOK, HEADS * HEAD), bf16),
            pltpu.VMEM((64, HEADS * HEAD), bf16),
            pltpu.VMEM((SEQ, 80, HEAD), bf16),
            pltpu.VMEM((TOKENS, HEAD), bf16),
            pltpu.VMEM((TOKENS, HEAD), bf16),
            pltpu.VMEM((SEQ, 80, HEAD), bf16),
            pltpu.VMEM((TOKENS, 2 * HEAD), bf16),
            pltpu.VMEM((TOKENS, 2 * HEAD), bf16),
            pltpu.VMEM((TOKENS, HEAD), bf16),
            pltpu.VMEM((TOKENS, HEAD), f32),
            pltpu.VMEM((TOKENS, HEAD), f32),
            pltpu.VMEM((2, QB, KB), f32),
            pltpu.VMEM((2, QB, HEAD), f32),
            pltpu.VMEM((SEQ, 80, HEAD), bf16),
            pltpu.VMEM((SEQ, 80, HEAD), bf16),
            pltpu.SemaphoreType.DMA((5,)),
            pltpu.SemaphoreType.DMA((4,)),
            pltpu.SemaphoreType.DMA((NQ,)),
            pltpu.SemaphoreType.DMA((NK,)),
            pltpu.SemaphoreType.DMA((NK,)),
            pltpu.SemaphoreType.DMA,
            pltpu.VMEM((FRAMES, 4, LCOLS * LAT_CH), bf16),
            pltpu.VMEM((LCOLS * 16, HEAD), f32),
            pltpu.VMEM((9, 48, CH), bf16),
            pltpu.VMEM((8, 80, HEAD), f32),
            pltpu.VMEM((FRAMES * 8, 56, HEAD), f32),
            pltpu.VMEM((4, 48, HEAD), f32),
            pltpu.VMEM((2, 48, HEAD), bf16),
            pltpu.VMEM((2, 48, HEAD), bf16),
            pltpu.VMEM((2, 2, 48, HEAD), bf16),
            pltpu.VMEM((FRAMES, 240, 640), bf16),
            pltpu.VMEM((640, CH), bf16),
            pltpu.VMEM((FRAMES, TOK, CH), f32),
            pltpu.VMEM((FRAMES * 6, 56, CH), f32),
            pltpu.VMEM((FRAMES, TOK, 9 * CH), bf16),
            pltpu.VMEM((FRAMES, 240, HEAD), f32),
            pltpu.VMEM((3, 9 * CH, CH), bf16),
            pltpu.VMEM((FRAMES, TOK, CH), bf16),
            pltpu.VMEM((FRAMES, 80, CH), bf16),
            pltpu.SemaphoreType.DMA((2,)),
            pltpu.SemaphoreType.DMA((2,)),
            pltpu.SemaphoreType.DMA((2,)),
        ],
        compiler_params=pltpu.CompilerParams(
            collective_id=1, has_side_effects=True, vmem_limit_bytes=58 * 2**20
        ),
        cost_estimate=pl.CostEstimate(
            flops=4 * TOKENS * TOKENS * HEAD, bytes_accessed=24 * 2**20,
            transcendentals=TOKENS * TOKENS,
        ),
        name="clip",
    )(
        query, key, value, head_weight.T, latent, conv_in.reshape(9, 48, CH),
        conv_mid.reshape(3, 9 * CH, CH), gamma.reshape(1, CH), band_rows,
    )


def per_device(query, key, value, latent, band_rows, head_weight, conv_in, conv_mid, gamma):
    rows = decode_clip(
        query, key, value, latent, band_rows, head_weight, conv_in, conv_mid, gamma
    )
    return rows.reshape(FRAMES, 3 * BAND, LCOLS, CH)


def solution(mesh):
    return jax.shard_map(
        per_device,
        mesh=mesh,
        in_specs=(
            P(("rep", "seq"), None),
            P(("rep", "seq"), None),
            P(("rep", "seq"), None),
            P("rep", "seq", None),
            P("rep"),
            P(),
            P(),
            P(),
            P(),
        ),
        out_specs=P("rep", "seq", None, None),
        check_vma=False,
    )
```

```python
import functools
import math

import jax
import jax.numpy as jnp
from jax import lax
from jax.experimental import pallas as pl
from jax.experimental.pallas import tpu as pltpu
from jax.sharding import PartitionSpec as P

HEADS = 32
HEAD = 128
LAT_CH = 16
CH = 384
FRAMES = 4
BAND = 2
PCOLS = 20
LCOLS = 40
TOK = 160
TOKENS = 5120
SEQ = 32
QB = 640
KB = 1280
NQ = TOKENS // QB
NK = TOKENS // KB
SCALE = math.log2(math.e) / math.sqrt(HEAD)
NEG = -1e30
V_AFTER = 1
MID_AT = 14

CHIPS = (
    (0, 0), (1, 1), (3, 3), (2, 2), (1, 3), (3, 1), (2, 0), (0, 2),
    (1, 0), (3, 2), (0, 1), (2, 3), (3, 0), (1, 2), (0, 3), (2, 1),
)
ARRIVE = ("K0", "Q0", "Q1", "K1", "Q2", "Q3", "Q4", "K2", "Q5", "Q6", "K3", "Q7")


def plan_tiles():
    keys, queries, tiles = [], [], []
    for name in ARRIVE:
        place = int(name[1])
        if name[0] == "K":
            fresh = [(q, place) for q in queries]
            keys.append(place)
        else:
            fresh = [(place, k) for k in keys]
            queries.append(place)
        tiles += fresh
    seen_q, seen_k, rows = set(), set(), []
    for t, (q, k) in enumerate(tiles):
        last = all(u[0] != q for u in tiles[t + 1:])
        rows.append((q, k, int(q not in seen_q), int(k not in seen_k), int(last)))
        seen_q.add(q)
        seen_k.add(k)
    return rows


TILES = plan_tiles()


def packed_table(values, bits):
    per = 24 // bits
    words = []
    for at in range(0, len(values), per):
        word = 0
        for i, value in enumerate(values[at:at + per]):
            word |= value << (bits * i)
        words.append(word)

    def look(index):
        word = jnp.int32(words[0])
        for i in range(1, len(words)):
            word = jnp.where(index >= i * per, jnp.int32(words[i]), word)
        shift = lax.rem(index, per) * bits
        return lax.shift_right_logical(word, shift) & ((1 << bits) - 1)

    return look


def clip_kernel(
    q_hbm, k_hbm, v_hbm, w_hbm, lat_hbm, first_hbm, mid_hbm, gamma_hbm, band_hbm, out_ref,
    v_in, w_in, v_send, q_got, k_got, v_got, q2, k2, v2, acc_ref, top_ref, s_ref, tile_top,
    y_send, y_got, in_sem, send_sem, q_sem, k_sem, v_sem, y_sem,
    lat_in, lat, w_first, turned, win, own, above, below, near, first_in, w1, first, wide, taps,
    total, w2, mine, extra, halo_ssem, halo_rsem, pair_sem,
    gamma_in, band_in,
):
    bf16, f32 = jnp.bfloat16, jnp.float32
    me = lax.axis_index("seq")
    my_x, my_z, my_c = me // 8, lax.rem(me // 2, 4), lax.rem(me, 2)
    look_dx = packed_table([c[0] for c in CHIPS], 2)
    look_dz = packed_table([c[1] for c in CHIPS], 2)

    def ahead(j):
        chip = j // 2
        x = lax.rem(my_x + look_dx(chip), 4)
        z = lax.rem(my_z + look_dz(chip), 4)
        return x * 8 + z * 2 + lax.rem(my_c + j, 2)

    def behind(j):
        chip = j // 2
        x = lax.rem(my_x + 4 - look_dx(chip), 4)
        z = lax.rem(my_z + 4 - look_dz(chip), 4)
        return x * 8 + z * 2 + lax.rem(my_c + j, 2)

    def head_cols(h):
        return pl.ds(pl.multiple_of(h * HEAD, HEAD), HEAD)

    def slot_rows(j):
        return pl.ds(pl.multiple_of(j * TOK, 32), TOK)

    def push(source, target, to, which, sem):
        pltpu.make_async_remote_copy(
            src_ref=source, dst_ref=target, send_sem=send_sem.at[which], recv_sem=sem,
            device_id={"seq": to}, device_id_type=pl.DeviceIdType.MESH,
        ).start()

    def arrived(ref, sem):
        pltpu.make_async_copy(ref, ref, sem).wait()

    v_load = pltpu.make_async_copy(v_hbm, v_in, in_sem.at[0])
    w_load = pltpu.make_async_copy(w_hbm, w_in, in_sem.at[1])
    v_load.start()
    w_load.start()
    pltpu.make_async_copy(k_hbm.at[:, head_cols(me)], k_got.at[pl.ds(0, TOK)], k_sem.at[0]).start()
    pltpu.make_async_copy(q_hbm.at[:, head_cols(me)], q_got.at[pl.ds(0, TOK)], q_sem.at[0]).start()
    barrier = pltpu.get_barrier_semaphore()

    def greet(j, carry):
        pl.semaphore_signal(
            barrier, inc=1, device_id={"seq": ahead(j)}, device_id_type=pl.DeviceIdType.MESH
        )
        return carry

    lax.fori_loop(1, SEQ, greet, 0)
    pl.semaphore_wait(barrier, SEQ - 1)

    def send_k(j, carry):
        to = ahead(j)
        push(k_hbm.at[:, head_cols(to)], k_got.at[slot_rows(j)], to, 0, k_sem.at[j // 8])
        return carry

    def send_q(j, carry):
        to = ahead(j)
        push(q_hbm.at[:, head_cols(to)], q_got.at[slot_rows(j)], to, 1, q_sem.at[j // 4])
        return carry

    def send_v(j, carry):
        push(v_send.at[j], v_got.at[j], ahead(j), 2, v_sem.at[j // 8])
        return carry

    def project(j, carry):
        h = ahead(j)
        y = lax.dot_general(
            v_in[:, head_cols(h)], w_in[:, head_cols(h)],
            (((1,), (1,)), ((), ())), preferred_element_type=jnp.float32,
        )
        v_send[j] = jnp.concatenate([y[:80], y[80:]], axis=1).astype(jnp.bfloat16)
        return carry

    pending = []
    for at, name in enumerate(ARRIVE):
        place = int(name[1])
        if name[0] == "K":
            lax.fori_loop(max(1, place * 8), place * 8 + 8, send_k, 0)
            pending.append(place)
        else:
            lax.fori_loop(max(1, place * 4), place * 4 + 4, send_q, 0)
        if at >= V_AFTER and pending:
            if pending[0] == 0:
                v_load.wait()
                w_load.wait()
            for chunk in pending:
                lax.fori_loop(chunk * 8, chunk * 8 + 8, project, 0, unroll=4)
                lax.fori_loop(max(1, chunk * 8), chunk * 8 + 8, send_v, 0)
            if pending[0] == 0:
                pltpu.make_async_copy(v_send.at[0], v_got.at[0], v_sem.at[0]).start()
            pending = []

    lat_load = pltpu.make_async_copy(lat_hbm, lat_in, in_sem.at[2])
    first_load = pltpu.make_async_copy(first_hbm, w_first, in_sem.at[3])
    mid_load = pltpu.make_async_copy(mid_hbm, w2, in_sem.at[4])
    gamma_load = pltpu.make_async_copy(gamma_hbm, gamma_in, in_sem.at[5])
    band_load = pltpu.make_async_copy(band_hbm, band_in, in_sem.at[6])
    lat_load.start()
    first_load.start()
    gamma_load.start()
    band_load.start()
    win[...] = jnp.zeros_like(win)
    wide[:, 0:8, :] = jnp.zeros((FRAMES * 6, 8, CH), f32)
    wide[:, 48:56, :] = jnp.zeros((FRAMES * 6, 8, CH), f32)
    own[:, LCOLS:, :] = jnp.zeros((4, 8, HEAD), f32)
    blank = jnp.zeros((240, HEAD), bf16)
    first_in[0, :, 0:128] = blank
    first_in[0, :, 128:256] = blank
    first_in[1, :, 0:128] = blank
    first_in[0, :, 384:512] = blank
    lat_load.wait()
    flat = jnp.concatenate([lat_in[f].astype(f32) for f in range(FRAMES)], axis=0)
    for block in range(5):
        lanes = flat[:, block * HEAD:(block + 1) * HEAD]
        for u in range(8):
            x = block * 8 + u
            lat[x * 16:(x + 1) * 16, :] = lanes if u == 0 else pltpu.roll(lanes, HEAD - LAT_CH * u, 1)
    gamma_load.wait()
    band_load.wait()
    w1[...] = jnp.zeros_like(w1)
    first_load.wait()
    for s in range(3):
        w1[s * HEAD:s * HEAD + 48, :] = w_first[s * 3]
        w1[s * HEAD + 64:s * HEAD + 112, :] = w_first[s * 3 + 1]
    w1[384:432, :] = w_first[2]
    w1[448:496, :] = w_first[5]
    w1[512:560, :] = w_first[8]

    def q_rows(i):
        return pl.ds(pl.multiple_of(i * QB, QB), QB)

    def k_rows(i):
        return pl.ds(pl.multiple_of(i * KB, KB), KB)

    def prep_q(i):
        rows = q_rows(i)
        arrived(q_got.at[rows], q_sem.at[i])
        scaled = q_got[rows, :].astype(jnp.float32) * SCALE
        high = scaled.astype(jnp.bfloat16)
        q2[rows, :HEAD] = high
        q2[rows, HEAD:] = (scaled - high.astype(jnp.float32)).astype(jnp.bfloat16)
        acc_ref[rows, :] = jnp.zeros((QB, HEAD), jnp.float32)
        top_ref[rows, :] = jnp.full((QB, HEAD), NEG, jnp.float32)

    def prep_k(i):
        lane = lax.broadcasted_iota(jnp.int32, (80, HEAD), 1)
        ones = jnp.where(lane == 64, 1.0, 0.0)
        rows = k_rows(i)
        arrived(k_got.at[rows], k_sem.at[i])
        k2[rows, :HEAD] = k_got[rows, :]
        k2[rows, HEAD:] = k_got[rows, :]
        slots = pl.ds(pl.multiple_of(i * 8, 8), 8)
        arrived(v_got.at[slots], v_sem.at[i])
        for u in range(8):
            j = i * 8 + u
            both = v_got[j].astype(jnp.float32)
            left = jnp.where(lane < 64, both, ones)
            right = jnp.where(lane < 64, pltpu.roll(both, 64, 1), ones)
            at = pl.multiple_of(j * TOK, 32)
            v2[pl.ds(at, 80), :] = left.astype(jnp.bfloat16)
            v2[pl.ds(at + 80, 80), :] = right.astype(jnp.bfloat16)

    def finish(i):
        rows = q_rows(i)
        total = acc_ref[rows, :]
        y = total * (1.0 / total[:, 64:65])
        for u in range(4):
            j = i * 4 + u
            part = y[u * TOK:(u + 1) * TOK]
            merged = jnp.where(
                lax.broadcasted_iota(jnp.int32, (80, HEAD), 1) < 64,
                part[:80], pltpu.roll(part[80:], 64, 1),
            )
            y_send[j] = merged.astype(jnp.bfloat16)

        def one(u, carry):
            j = i * 4 + u

            @pl.when(j > 0)
            def _():
                push(y_send.at[j], y_got.at[j], behind(j), 3, y_sem)

            return carry

        lax.fori_loop(0, 4, one, 0)

    look_q = packed_table([t[0] for t in TILES], 3)
    look_k = packed_table([t[1] for t in TILES], 2)
    look_new_q = packed_table([t[2] for t in TILES], 1)
    look_new_k = packed_table([t[3] for t in TILES], 1)
    look_last = packed_table([t[4] for t in TILES], 1)

    def ready(t):
        @pl.when(look_new_k(t) == 1)
        def _():
            prep_k(look_k(t))

        @pl.when(look_new_q(t) == 1)
        def _():
            prep_q(look_q(t))

    def score(t, slot):
        s = lax.dot_general(
            q2[q_rows(look_q(t)), :], k2[k_rows(look_k(t)), :],
            (((1,), (1,)), ((), ())), preferred_element_type=jnp.float32,
        )
        s_ref[slot] = s
        top = s[:, :HEAD]
        for u in range(1, KB // HEAD):
            top = jnp.maximum(top, s[:, u * HEAD:(u + 1) * HEAD])
        tile_top[slot] = top

    def weigh(t, slot):
        rows = q_rows(look_q(t))
        before = top_ref[rows, :]
        now = jnp.maximum(before, jnp.max(tile_top[slot], axis=1, keepdims=True))
        top_ref[rows, :] = now
        weights = jnp.exp2(s_ref[slot] - jnp.concatenate([now] * (KB // HEAD), axis=1))
        acc_ref[rows, :] = acc_ref[rows, :] * jnp.exp2(before - now) + jnp.dot(
            weights.astype(jnp.bfloat16), v2[k_rows(look_k(t)), :],
            preferred_element_type=jnp.float32,
        )

    def after(t):
        @pl.when(t == MID_AT)
        def _():
            mid_load.start()

        @pl.when(look_last(t) == 1)
        def _():
            finish(look_q(t))

    def step(t, slot):
        ready(t + 1)
        score(t + 1, 1 - slot)
        weigh(t, slot)
        after(t)

    def two_steps(i, carry):
        step(2 * i, 0)
        step(2 * i + 1, 1)
        return carry

    count = len(TILES)
    ready(jnp.int32(0))
    score(jnp.int32(0), 0)
    lax.fori_loop(0, (count - 2) // 2, two_steps, 0)
    step(jnp.int32(count - 2), 0)
    weigh(jnp.int32(count - 1), 1)
    after(jnp.int32(count - 1))

    others = pl.ds(1, SEQ - 1)
    arrived(y_got.at[others], y_sem)

    def gather(j, total):
        return total + y_got[j].astype(jnp.float32)

    vel = lax.fori_loop(1, SEQ, gather, y_send[0].astype(f32), unroll=True)
    up, down = lax.rem(me + SEQ - 1, SEQ), lax.rem(me + 1, SEQ)
    odd = lax.rem(me, 2)
    lane40 = lax.broadcasted_iota(jnp.int32, (LCOLS, HEAD), 1)
    lane20 = lax.broadcasted_iota(jnp.int32, (80, HEAD), 1)
    for o in range(8):
        turn = vel if o == 0 else pltpu.roll(vel, HEAD - LAT_CH * o, 1)
        turned[o] = jnp.where(lane20 < LAT_CH, turn, 0.0)
    for f in range(FRAMES):
        for r in range(BAND):
            for a in range(2):
                for b in range(2):
                    o = (f // 2) * 4 + a * 2 + b
                    row = f * 8 + 2 + 2 * r + a
                    win[row, pl.ds(8 + b, PCOLS, stride=2), :] = turned[
                        o, pl.ds(((f % 2) * BAND + r) * PCOLS, PCOLS), :
                    ]
    for y in range(4):
        merged = jnp.zeros((LCOLS, HEAD), f32)
        for f in range(FRAMES):
            grid = win[f * 8 + 2 + y, 8:48, :]
            clean = (lat[pl.ds(f * 4 + y, LCOLS, stride=16), :] - 0.9 * grid).astype(bf16).astype(f32)
            clean = jnp.where(lane40 < LAT_CH, clean, 0.0)
            win[f * 8 + 2 + y, 8:48, :] = clean
            merged = merged + (clean if f == 0 else pltpu.roll(clean, LAT_CH * f, 1))
        own[y, 0:LCOLS, :] = merged
    near[0] = own[0:2].astype(bf16)
    near[1] = own[2:4].astype(bf16)
    to_up = pltpu.make_async_remote_copy(
        src_ref=near.at[0], dst_ref=below, send_sem=halo_ssem.at[0], recv_sem=halo_rsem.at[0],
        device_id={"seq": up}, device_id_type=pl.DeviceIdType.MESH,
    )
    to_down = pltpu.make_async_remote_copy(
        src_ref=near.at[1], dst_ref=above, send_sem=halo_ssem.at[1], recv_sem=halo_rsem.at[1],
        device_id={"seq": down}, device_id_type=pl.DeviceIdType.MESH,
    )
    to_up.start()
    to_down.start()

    to_up.wait_recv()
    to_down.wait_recv()
    for side in range(2):
        there = (me > 0) if side == 0 else (me < SEQ - 1)
        got = above if side == 0 else below
        for y in range(2):
            rows = jnp.where(there, got[y, 0:LCOLS, :].astype(f32), 0.0)
            for f in range(FRAMES):
                part = rows if f == 0 else pltpu.roll(rows, HEAD - LAT_CH * f, 1)
                win[f * 8 + (0 if side == 0 else 6) + y, 8:48, :] = jnp.where(
                    lane40 < LAT_CH, part, 0.0
                )

    def gather_columns(f, carry):
        parts = []
        for y in range(8):
            row = f * 8 + y
            parts.append(
                win[row, 7:47, :]
                + pltpu.roll(win[row, 8:48, :], LAT_CH, 1)
                + pltpu.roll(win[row, 9:49, :], 2 * LAT_CH, 1)
            )
        block = jnp.concatenate(parts, axis=0)
        pair = block[0:240] + pltpu.roll(block[40:280], 64, 1)
        single = block[80:320]
        first_in[f, :, 256:384] = pair.astype(bf16)
        first_in[f, :, 512:640] = single.astype(bf16)
        for later in (1, 2):
            @pl.when(f + later < FRAMES)
            def _():
                first_in[f + later, :, (2 - later) * HEAD:(3 - later) * HEAD] = pair.astype(bf16)

        total[f] = single
        return carry

    lax.fori_loop(0, FRAMES, gather_columns, 0)
    first_in[1, :, 384:512] = pltpu.roll(total[0], 64, 1).astype(bf16)
    first_in[2, :, 384:512] = (total[0] + pltpu.roll(total[1], 64, 1)).astype(bf16)
    first_in[3, :, 384:512] = (total[1] + pltpu.roll(total[2], 64, 1)).astype(bf16)

    def first_step(f, carry):
        conv = jnp.dot(first_in[f], w1[...], preferred_element_type=f32)
        values = conv.astype(bf16).astype(f32)
        power = jnp.mean(values * values, axis=1, keepdims=True)
        normed = values * lax.rsqrt(power + 1e-06) * gamma_in[...].reshape(1, CH)
        normed = normed / (1.0 + jnp.exp(-normed))
        place = lax.broadcasted_iota(jnp.int32, (240, CH), 0)
        outside = ((place < 40) & (me == 0)) | ((place >= 200) & (me == SEQ - 1))
        normed = jnp.where(outside, 0.0, normed)
        first[f] = values[40:200]
        for y in range(6):
            wide[f * 6 + y, 8:48, :] = normed[y * 40:(y + 1) * 40]
        for u in range(3):
            for w in range(3):
                rows = [wide[f * 6 + y + u, 7 + w:47 + w, :] for y in range(4)]
                at = (u * 3 + w) * CH
                taps[f, :, at:at + CH] = jnp.concatenate(rows, axis=0).astype(bf16)
        return carry

    lax.fori_loop(0, FRAMES, first_step, 0)
    mid_load.wait()
    for s in (2, 1, 0):
        count = FRAMES - (2 - s)
        for part in range(3):
            cols = slice(part * 3 * CH, (part + 1) * 3 * CH)
            term = jnp.dot(
                taps[0:count, :, cols].reshape(count * TOK, 3 * CH), w2[s, cols, :],
                preferred_element_type=f32,
            ).reshape(count, TOK, CH)
            first[2 - s:FRAMES] = first[2 - s:FRAMES] + term

    mine[...] = first[...].astype(bf16)
    hand = pltpu.make_async_remote_copy(
        src_ref=mine.at[:, pl.ds(0, 80), :], dst_ref=extra,
        send_sem=pair_sem.at[0], recv_sem=pair_sem.at[1],
        device_id={"seq": me - odd}, device_id_type=pl.DeviceIdType.MESH,
    )

    @pl.when(odd == 1)
    def _():
        hand.start()

    length = band_in[me]
    lead = odd * (2 * BAND - length)
    for f in range(FRAMES):
        for i in range(4):
            row = first[f, i * LCOLS:(i + 1) * LCOLS, :]
            for later in (1, 2):
                if i + later < 4:
                    at = (i + later) * LCOLS
                    row = jnp.where(lead == later, first[f, at:at + LCOLS, :], row)
            row = jnp.where(i < length, row, 0.0)
            out_ref[f, i * LCOLS:(i + 1) * LCOLS, :] = row.astype(bf16)

    @pl.when(odd == 1)
    def _():
        hand.wait_send()
        out_ref[:, TOK:TOK + 80, :] = jnp.zeros((FRAMES, 80, CH), bf16)

    @pl.when(odd == 0)
    def _():
        hand.wait_recv()
        for f in range(FRAMES):
            got = extra[f].astype(f32)
            place = lax.broadcasted_iota(jnp.int32, (80, CH), 0)
            got = jnp.where(place < (length - 4) * LCOLS, got, 0.0)
            out_ref[f, TOK:TOK + 80, :] = got.astype(bf16)

    to_up.wait_send()
    to_down.wait_send()
    arrived(k_got.at[pl.ds(TOK, TOKENS - TOK)], send_sem.at[0])
    arrived(q_got.at[pl.ds(TOK, TOKENS - TOK)], send_sem.at[1])
    arrived(v_got.at[others], send_sem.at[2])
    arrived(y_got.at[others], send_sem.at[3])


def decode_clip(query, key, value, latent, band_rows, head_weight, conv_in, conv_mid, gamma):
    bf16, f32 = jnp.bfloat16, jnp.float32
    any_space = pl.BlockSpec(memory_space=pltpu.HBM)
    vmem = pl.BlockSpec(memory_space=pltpu.VMEM)
    return pl.pallas_call(
        clip_kernel,
        out_shape=jax.ShapeDtypeStruct((FRAMES, TOK + 80, CH), bf16),
        in_specs=[any_space] * 9,
        out_specs=vmem,
        scratch_shapes=[
            pltpu.VMEM((TOK, HEADS * HEAD), bf16),
            pltpu.VMEM((64, HEADS * HEAD), bf16),
            pltpu.VMEM((SEQ, 80, HEAD), bf16),
            pltpu.VMEM((TOKENS, HEAD), bf16),
            pltpu.VMEM((TOKENS, HEAD), bf16),
            pltpu.VMEM((SEQ, 80, HEAD), bf16),
            pltpu.VMEM((TOKENS, 2 * HEAD), bf16),
            pltpu.VMEM((TOKENS, 2 * HEAD), bf16),
            pltpu.VMEM((TOKENS, HEAD), bf16),
            pltpu.VMEM((TOKENS, HEAD), f32),
            pltpu.VMEM((TOKENS, HEAD), f32),
            pltpu.VMEM((2, QB, KB), f32),
            pltpu.VMEM((2, QB, HEAD), f32),
            pltpu.VMEM((SEQ, 80, HEAD), bf16),
            pltpu.VMEM((SEQ, 80, HEAD), bf16),
            pltpu.SemaphoreType.DMA((7,)),
            pltpu.SemaphoreType.DMA((4,)),
            pltpu.SemaphoreType.DMA((NQ,)),
            pltpu.SemaphoreType.DMA((NK,)),
            pltpu.SemaphoreType.DMA((NK,)),
            pltpu.SemaphoreType.DMA,
            pltpu.VMEM((FRAMES, 4, LCOLS * LAT_CH), bf16),
            pltpu.VMEM((LCOLS * 16, HEAD), f32),
            pltpu.VMEM((9, 48, CH), bf16),
            pltpu.VMEM((8, 80, HEAD), f32),
            pltpu.VMEM((FRAMES * 8, 56, HEAD), f32),
            pltpu.VMEM((4, 48, HEAD), f32),
            pltpu.VMEM((2, 48, HEAD), bf16),
            pltpu.VMEM((2, 48, HEAD), bf16),
            pltpu.VMEM((2, 2, 48, HEAD), bf16),
            pltpu.VMEM((FRAMES, 240, 640), bf16),
            pltpu.VMEM((640, CH), bf16),
            pltpu.VMEM((FRAMES, TOK, CH), f32),
            pltpu.VMEM((FRAMES * 6, 56, CH), f32),
            pltpu.VMEM((FRAMES, TOK, 9 * CH), bf16),
            pltpu.VMEM((FRAMES, 240, HEAD), f32),
            pltpu.VMEM((3, 9 * CH, CH), bf16),
            pltpu.VMEM((FRAMES, TOK, CH), bf16),
            pltpu.VMEM((FRAMES, 80, CH), bf16),
            pltpu.SemaphoreType.DMA((2,)),
            pltpu.SemaphoreType.DMA((2,)),
            pltpu.SemaphoreType.DMA((2,)),
            pltpu.VMEM((CH,), f32),
            pltpu.SMEM((SEQ,), jnp.int32),
        ],
        compiler_params=pltpu.CompilerParams(
            collective_id=1, has_side_effects=True, vmem_limit_bytes=56 * 2**20
        ),
        cost_estimate=pl.CostEstimate(
            flops=4 * TOKENS * TOKENS * HEAD, bytes_accessed=24 * 2**20,
            transcendentals=TOKENS * TOKENS,
        ),
        name="clip",
    )(
        query, key, value, head_weight.T, latent, conv_in.reshape(9, 48, CH),
        conv_mid.reshape(3, 9 * CH, CH), gamma, band_rows,
    )


def per_device(query, key, value, latent, band_rows, head_weight, conv_in, conv_mid, gamma):
    rows = decode_clip(
        query, key, value, latent, band_rows, head_weight, conv_in, conv_mid, gamma
    )
    return rows.reshape(FRAMES, 3 * BAND, LCOLS, CH)


def solution(mesh):
    return jax.shard_map(
        per_device,
        mesh=mesh,
        in_specs=(
            P(("rep", "seq"), None),
            P(("rep", "seq"), None),
            P(("rep", "seq"), None),
            P("rep", "seq", None),
            P("rep"),
            P(),
            P(),
            P(),
            P(),
        ),
        out_specs=P("rep", "seq", None, None),
        check_vma=False,
    )
```

```python
import functools
import math

import jax
import jax.numpy as jnp
from jax import lax
from jax.experimental import pallas as pl
from jax.experimental.pallas import tpu as pltpu
from jax.sharding import PartitionSpec as P

HEADS = 32
HEAD = 128
LAT_CH = 16
CH = 384
FRAMES = 4
BAND = 2
PCOLS = 20
LCOLS = 40
TOK = 160
TOKENS = 5120
SEQ = 32
QB = 640
KB = 1280
NQ = TOKENS // QB
NK = TOKENS // KB
SCALE = math.log2(math.e) / math.sqrt(HEAD)
NEG = -1e30
V_AFTER = 1
MID_AT = 14

CHIPS = (
    (0, 0), (1, 1), (3, 3), (2, 2), (1, 3), (3, 1), (2, 0), (0, 2),
    (1, 0), (3, 2), (0, 1), (2, 3), (3, 0), (1, 2), (0, 3), (2, 1),
)
ARRIVE = ("K0", "Q0", "Q1", "K1", "Q2", "Q3", "Q4", "K2", "Q5", "Q6", "K3", "Q7")


def plan_tiles():
    keys, queries, tiles = [], [], []
    for name in ARRIVE:
        place = int(name[1])
        if name[0] == "K":
            fresh = [(q, place) for q in queries]
            keys.append(place)
        else:
            fresh = [(place, k) for k in keys]
            queries.append(place)
        tiles += fresh
    seen_q, seen_k, rows = set(), set(), []
    for t, (q, k) in enumerate(tiles):
        last = all(u[0] != q for u in tiles[t + 1:])
        rows.append((q, k, int(q not in seen_q), int(k not in seen_k), int(last)))
        seen_q.add(q)
        seen_k.add(k)
    return rows


TILES = plan_tiles()


def packed_table(values, bits):
    per = 24 // bits
    words = []
    for at in range(0, len(values), per):
        word = 0
        for i, value in enumerate(values[at:at + per]):
            word |= value << (bits * i)
        words.append(word)

    def look(index):
        word = jnp.int32(words[0])
        for i in range(1, len(words)):
            word = jnp.where(index >= i * per, jnp.int32(words[i]), word)
        shift = lax.rem(index, per) * bits
        return lax.shift_right_logical(word, shift) & ((1 << bits) - 1)

    return look


def clip_kernel(
    q_hbm, k_hbm, v_hbm, w_hbm, lat_hbm, first_hbm, mid_hbm, gamma_hbm, band_hbm, out_ref,
    v_in, w_in, v_send, q_got, k_got, v_got, q2, k2, v2, acc_ref, top_ref, s_ref, tile_top,
    y_send, y_got, in_sem, send_sem, q_sem, k_sem, v_sem, y_sem,
    lat_in, lat, w_first, turned, win, own, above, below, near, first_in, w1, first, wide, taps,
    total, w2, w3, w4, mine, extra, halo_ssem, halo_rsem, pair_sem,
    gamma_in, band_in,
):
    bf16, f32 = jnp.bfloat16, jnp.float32
    me = lax.axis_index("seq")
    my_x, my_z, my_c = me // 8, lax.rem(me // 2, 4), lax.rem(me, 2)
    look_dx = packed_table([c[0] for c in CHIPS], 2)
    look_dz = packed_table([c[1] for c in CHIPS], 2)

    def ahead(j):
        chip = j // 2
        x = lax.rem(my_x + look_dx(chip), 4)
        z = lax.rem(my_z + look_dz(chip), 4)
        return x * 8 + z * 2 + lax.rem(my_c + j, 2)

    def behind(j):
        chip = j // 2
        x = lax.rem(my_x + 4 - look_dx(chip), 4)
        z = lax.rem(my_z + 4 - look_dz(chip), 4)
        return x * 8 + z * 2 + lax.rem(my_c + j, 2)

    def head_cols(h):
        return pl.ds(pl.multiple_of(h * HEAD, HEAD), HEAD)

    def slot_rows(j):
        return pl.ds(pl.multiple_of(j * TOK, 32), TOK)

    def push(source, target, to, which, sem):
        pltpu.make_async_remote_copy(
            src_ref=source, dst_ref=target, send_sem=send_sem.at[which], recv_sem=sem,
            device_id={"seq": to}, device_id_type=pl.DeviceIdType.MESH,
        ).start()

    def arrived(ref, sem):
        pltpu.make_async_copy(ref, ref, sem).wait()

    barrier = pltpu.get_barrier_semaphore()

    def greet(j, carry):
        pl.semaphore_signal(
            barrier, inc=1, device_id={"seq": ahead(j)}, device_id_type=pl.DeviceIdType.MESH
        )
        return carry

    lax.fori_loop(1, SEQ, greet, 0, unroll=True)
    v_load = pltpu.make_async_copy(v_hbm, v_in, in_sem.at[0])
    w_load = pltpu.make_async_copy(w_hbm, w_in, in_sem.at[1])
    v_load.start()
    w_load.start()
    pltpu.make_async_copy(k_hbm.at[:, head_cols(me)], k_got.at[pl.ds(0, TOK)], k_sem.at[0]).start()
    pltpu.make_async_copy(q_hbm.at[:, head_cols(me)], q_got.at[pl.ds(0, TOK)], q_sem.at[0]).start()
    pl.semaphore_wait(barrier, SEQ - 1)

    def send_k(j, carry):
        to = ahead(j)
        push(k_hbm.at[:, head_cols(to)], k_got.at[slot_rows(j)], to, 0, k_sem.at[j // 8])
        return carry

    def send_q(j, carry):
        to = ahead(j)
        push(q_hbm.at[:, head_cols(to)], q_got.at[slot_rows(j)], to, 1, q_sem.at[j // 4])
        return carry

    def send_v(j, carry):
        push(v_send.at[j], v_got.at[j], ahead(j), 2, v_sem.at[j // 8])
        return carry

    def project(j, carry):
        h = ahead(j)
        y = lax.dot_general(
            v_in[:, head_cols(h)], w_in[:, head_cols(h)],
            (((1,), (1,)), ((), ())), preferred_element_type=jnp.float32,
        )
        v_send[j] = jnp.concatenate([y[:80], y[80:]], axis=1).astype(jnp.bfloat16)
        return carry

    pending = []
    for at, name in enumerate(ARRIVE):
        place = int(name[1])
        if name[0] == "K":
            lax.fori_loop(max(1, place * 8), place * 8 + 8, send_k, 0, unroll=True)
            pending.append(place)
        else:
            lax.fori_loop(max(1, place * 4), place * 4 + 4, send_q, 0, unroll=True)
        if at >= V_AFTER and pending:
            if pending[0] == 0:
                v_load.wait()
                w_load.wait()
            for chunk in pending:
                lax.fori_loop(chunk * 8, chunk * 8 + 8, project, 0, unroll=4)
                lax.fori_loop(max(1, chunk * 8), chunk * 8 + 8, send_v, 0)
            if pending[0] == 0:
                pltpu.make_async_copy(v_send.at[0], v_got.at[0], v_sem.at[0]).start()
            pending = []

    lat_load = pltpu.make_async_copy(lat_hbm, lat_in, in_sem.at[2])
    first_load = pltpu.make_async_copy(first_hbm, w_first, in_sem.at[3])
    last = pl.ds(256, HEAD)
    mid_loads = [
        pltpu.make_async_copy(source, target, in_sem.at[4 + n])
        for n, (source, target) in enumerate((
            (mid_hbm.at[:, :, pl.ds(0, 256)], w2),
            (mid_hbm.at[2, :, last], w3.at[:, pl.ds(0, HEAD)]),
            (mid_hbm.at[1, :, last], w3.at[:, pl.ds(HEAD, HEAD)]),
            (mid_hbm.at[0, :, last], w4),
        ))
    ]
    gamma_load = pltpu.make_async_copy(gamma_hbm, gamma_in, in_sem.at[8])
    band_load = pltpu.make_async_copy(band_hbm, band_in, in_sem.at[9])
    lat_load.start()
    first_load.start()
    gamma_load.start()
    band_load.start()
    win[...] = jnp.zeros_like(win)
    wide[:, 0:8, :] = jnp.zeros((FRAMES * 6, 8, CH), f32)
    wide[:, 48:56, :] = jnp.zeros((FRAMES * 6, 8, CH), f32)
    own[:, LCOLS:, :] = jnp.zeros((4, 8, HEAD), f32)
    blank = jnp.zeros((240, HEAD), bf16)
    first_in[0, :, 0:128] = blank
    first_in[0, :, 128:256] = blank
    first_in[1, :, 0:128] = blank
    first_in[0, :, 384:512] = blank
    lat_load.wait()
    flat = jnp.concatenate([lat_in[f].astype(f32) for f in range(FRAMES)], axis=0)
    for block in range(5):
        lanes = flat[:, block * HEAD:(block + 1) * HEAD]
        for u in range(8):
            x = block * 8 + u
            lat[x * 16:(x + 1) * 16, :] = lanes if u == 0 else pltpu.roll(lanes, HEAD - LAT_CH * u, 1)
    gamma_load.wait()
    band_load.wait()
    w1[...] = jnp.zeros_like(w1)
    first_load.wait()
    for s in range(3):
        w1[s * HEAD:s * HEAD + 48, :] = w_first[s * 3]
        w1[s * HEAD + 64:s * HEAD + 112, :] = w_first[s * 3 + 1]
    w1[384:432, :] = w_first[2]
    w1[448:496, :] = w_first[5]
    w1[512:560, :] = w_first[8]

    def q_rows(i):
        return pl.ds(pl.multiple_of(i * QB, QB), QB)

    def k_rows(i):
        return pl.ds(pl.multiple_of(i * KB, KB), KB)

    def prep_q(i):
        rows = q_rows(i)
        arrived(q_got.at[rows], q_sem.at[i])
        scaled = q_got[rows, :].astype(jnp.float32) * SCALE
        high = scaled.astype(jnp.bfloat16)
        q2[rows, :HEAD] = high
        q2[rows, HEAD:] = (scaled - high.astype(jnp.float32)).astype(jnp.bfloat16)
        acc_ref[rows, :] = jnp.zeros((QB, HEAD), jnp.float32)
        top_ref[rows, :] = jnp.full((QB, HEAD), NEG, jnp.float32)

    def prep_k(i):
        lane = lax.broadcasted_iota(jnp.int32, (80, HEAD), 1)
        ones = jnp.where(lane == 64, 1.0, 0.0)
        rows = k_rows(i)
        arrived(k_got.at[rows], k_sem.at[i])
        k2[rows, :HEAD] = k_got[rows, :]
        k2[rows, HEAD:] = k_got[rows, :]
        slots = pl.ds(pl.multiple_of(i * 8, 8), 8)
        arrived(v_got.at[slots], v_sem.at[i])
        for u in range(8):
            j = i * 8 + u
            both = v_got[j].astype(jnp.float32)
            left = jnp.where(lane < 64, both, ones)
            right = jnp.where(lane < 64, pltpu.roll(both, 64, 1), ones)
            at = pl.multiple_of(j * TOK, 32)
            v2[pl.ds(at, 80), :] = left.astype(jnp.bfloat16)
            v2[pl.ds(at + 80, 80), :] = right.astype(jnp.bfloat16)

    def finish(i):
        rows = q_rows(i)
        total = acc_ref[rows, :]
        y = total * (1.0 / total[:, 64:65])
        for u in range(4):
            j = i * 4 + u
            part = y[u * TOK:(u + 1) * TOK]
            merged = jnp.where(
                lax.broadcasted_iota(jnp.int32, (80, HEAD), 1) < 64,
                part[:80], pltpu.roll(part[80:], 64, 1),
            )
            y_send[j] = merged.astype(jnp.bfloat16)

        def one(u, carry):
            j = i * 4 + u

            @pl.when(j > 0)
            def _():
                push(y_send.at[j], y_got.at[j], behind(j), 3, y_sem)

            return carry

        lax.fori_loop(0, 4, one, 0)

    look_q = packed_table([t[0] for t in TILES], 3)
    look_k = packed_table([t[1] for t in TILES], 2)
    look_new_q = packed_table([t[2] for t in TILES], 1)
    look_new_k = packed_table([t[3] for t in TILES], 1)
    look_last = packed_table([t[4] for t in TILES], 1)

    def ready(t):
        @pl.when(look_new_k(t) == 1)
        def _():
            prep_k(look_k(t))

        @pl.when(look_new_q(t) == 1)
        def _():
            prep_q(look_q(t))

    def score(t, slot):
        s = lax.dot_general(
            q2[q_rows(look_q(t)), :], k2[k_rows(look_k(t)), :],
            (((1,), (1,)), ((), ())), preferred_element_type=jnp.float32,
        )
        s_ref[slot] = s
        top = s[:, :HEAD]
        for u in range(1, KB // HEAD):
            top = jnp.maximum(top, s[:, u * HEAD:(u + 1) * HEAD])
        tile_top[slot] = top

    def weigh(t, slot):
        rows = q_rows(look_q(t))
        before = top_ref[rows, :]
        now = jnp.maximum(before, jnp.max(tile_top[slot], axis=1, keepdims=True))
        top_ref[rows, :] = now
        weights = jnp.exp2(s_ref[slot] - jnp.concatenate([now] * (KB // HEAD), axis=1))
        acc_ref[rows, :] = acc_ref[rows, :] * jnp.exp2(before - now) + jnp.dot(
            weights.astype(jnp.bfloat16), v2[k_rows(look_k(t)), :],
            preferred_element_type=jnp.float32,
        )

    def after(t):
        @pl.when(t == MID_AT)
        def _():
            for load in mid_loads:
                load.start()

        @pl.when(look_last(t) == 1)
        def _():
            finish(look_q(t))

    def step(t, slot):
        ready(t + 1)
        score(t + 1, 1 - slot)
        weigh(t, slot)
        after(t)

    def two_steps(i, carry):
        step(2 * i, 0)
        step(2 * i + 1, 1)
        return carry

    count = len(TILES)
    ready(jnp.int32(0))
    score(jnp.int32(0), 0)
    lax.fori_loop(0, (count - 2) // 2, two_steps, 0)
    step(jnp.int32(count - 2), 0)
    weigh(jnp.int32(count - 1), 1)
    after(jnp.int32(count - 1))

    others = pl.ds(1, SEQ - 1)
    arrived(y_got.at[others], y_sem)

    def gather(j, total):
        return total + y_got[j].astype(jnp.float32)

    vel = lax.fori_loop(1, SEQ, gather, y_send[0].astype(f32), unroll=True)
    up, down = lax.rem(me + SEQ - 1, SEQ), lax.rem(me + 1, SEQ)
    odd = lax.rem(me, 2)
    lane40 = lax.broadcasted_iota(jnp.int32, (LCOLS, HEAD), 1)
    lane20 = lax.broadcasted_iota(jnp.int32, (80, HEAD), 1)
    for o in range(8):
        turn = vel if o == 0 else pltpu.roll(vel, HEAD - LAT_CH * o, 1)
        turned[o] = jnp.where(lane20 < LAT_CH, turn, 0.0)
    for f in range(FRAMES):
        for r in range(BAND):
            for a in range(2):
                for b in range(2):
                    o = (f // 2) * 4 + a * 2 + b
                    row = f * 8 + 2 + 2 * r + a
                    win[row, pl.ds(8 + b, PCOLS, stride=2), :] = turned[
                        o, pl.ds(((f % 2) * BAND + r) * PCOLS, PCOLS), :
                    ]
    for y in range(4):
        merged = jnp.zeros((LCOLS, HEAD), f32)
        for f in range(FRAMES):
            grid = win[f * 8 + 2 + y, 8:48, :]
            clean = (lat[pl.ds(f * 4 + y, LCOLS, stride=16), :] - 0.9 * grid).astype(bf16).astype(f32)
            clean = jnp.where(lane40 < LAT_CH, clean, 0.0)
            win[f * 8 + 2 + y, 8:48, :] = clean
            merged = merged + (clean if f == 0 else pltpu.roll(clean, LAT_CH * f, 1))
        own[y, 0:LCOLS, :] = merged
    near[0] = own[0:2].astype(bf16)
    near[1] = own[2:4].astype(bf16)
    to_up = pltpu.make_async_remote_copy(
        src_ref=near.at[0], dst_ref=below, send_sem=halo_ssem.at[0], recv_sem=halo_rsem.at[0],
        device_id={"seq": up}, device_id_type=pl.DeviceIdType.MESH,
    )
    to_down = pltpu.make_async_remote_copy(
        src_ref=near.at[1], dst_ref=above, send_sem=halo_ssem.at[1], recv_sem=halo_rsem.at[1],
        device_id={"seq": down}, device_id_type=pl.DeviceIdType.MESH,
    )
    to_up.start()
    to_down.start()

    to_up.wait_recv()
    to_down.wait_recv()
    for side in range(2):
        there = (me > 0) if side == 0 else (me < SEQ - 1)
        got = above if side == 0 else below
        for y in range(2):
            rows = jnp.where(there, got[y, 0:LCOLS, :].astype(f32), 0.0)
            for f in range(FRAMES):
                part = rows if f == 0 else pltpu.roll(rows, HEAD - LAT_CH * f, 1)
                win[f * 8 + (0 if side == 0 else 6) + y, 8:48, :] = jnp.where(
                    lane40 < LAT_CH, part, 0.0
                )

    def gather_columns(f, carry):
        parts = []
        for y in range(8):
            row = f * 8 + y
            parts.append(
                win[row, 7:47, :]
                + pltpu.roll(win[row, 8:48, :], LAT_CH, 1)
                + pltpu.roll(win[row, 9:49, :], 2 * LAT_CH, 1)
            )
        block = jnp.concatenate(parts, axis=0)
        pair = block[0:240] + pltpu.roll(block[40:280], 64, 1)
        single = block[80:320]
        first_in[f, :, 256:384] = pair.astype(bf16)
        first_in[f, :, 512:640] = single.astype(bf16)
        for later in (1, 2):
            @pl.when(f + later < FRAMES)
            def _():
                first_in[f + later, :, (2 - later) * HEAD:(3 - later) * HEAD] = pair.astype(bf16)

        total[f] = single
        return carry

    lax.fori_loop(0, FRAMES, gather_columns, 0)
    first_in[1, :, 384:512] = pltpu.roll(total[0], 64, 1).astype(bf16)
    first_in[2, :, 384:512] = (total[0] + pltpu.roll(total[1], 64, 1)).astype(bf16)
    first_in[3, :, 384:512] = (total[1] + pltpu.roll(total[2], 64, 1)).astype(bf16)

    def first_step(f, carry):
        conv = jnp.dot(first_in[f], w1[...], preferred_element_type=f32)
        values = conv.astype(bf16).astype(f32)
        power = jnp.mean(values * values, axis=1, keepdims=True)
        normed = values * lax.rsqrt(power + 1e-06) * gamma_in[...].reshape(1, CH)
        normed = normed / (1.0 + jnp.exp(-normed))
        place = lax.broadcasted_iota(jnp.int32, (240, CH), 0)
        outside = ((place < 40) & (me == 0)) | ((place >= 200) & (me == SEQ - 1))
        normed = jnp.where(outside, 0.0, normed)
        first[f] = values[40:200]
        for y in range(6):
            wide[f * 6 + y, 8:48, :] = normed[y * 40:(y + 1) * 40]
        for u in range(3):
            for w in range(3):
                rows = [wide[f * 6 + y + u, 7 + w:47 + w, :] for y in range(4)]
                at = (u * 3 + w) * CH
                taps[f, :, at:at + CH] = jnp.concatenate(rows, axis=0).astype(bf16)
        return carry

    lax.fori_loop(0, FRAMES, first_step, 0)
    for load in mid_loads:
        load.wait()

    def product(count, weights):
        source = taps[0:count].reshape(count * TOK, 9 * CH)
        return sum(
            jnp.dot(source[:, low:high], weights[low:high, :], preferred_element_type=f32)
            for low, high in ((0, 1280), (1280, 2560), (2560, 3456))
        ).reshape(count, TOK, -1)

    for s in (2, 1, 0):
        first[2 - s:FRAMES, :, 0:256] = first[2 - s:FRAMES, :, 0:256] + product(2 + s, w2.at[s])
    term = product(FRAMES, w3)
    first[:, :, 256:CH] = first[:, :, 256:CH] + term[:, :, 0:HEAD]
    first[1:FRAMES, :, 256:CH] = first[1:FRAMES, :, 256:CH] + term[0:FRAMES - 1, :, HEAD:]
    first[2:FRAMES, :, 256:CH] = first[2:FRAMES, :, 256:CH] + product(2, w4)
    mine[...] = first[...].astype(bf16)
    hand = pltpu.make_async_remote_copy(
        src_ref=mine.at[:, pl.ds(0, 80), :], dst_ref=extra,
        send_sem=pair_sem.at[0], recv_sem=pair_sem.at[1],
        device_id={"seq": me - odd}, device_id_type=pl.DeviceIdType.MESH,
    )

    @pl.when(odd == 1)
    def _():
        hand.start()

    length = band_in[me]
    lead = odd * (2 * BAND - length)
    for f in range(FRAMES):
        for i in range(4):
            row = first[f, i * LCOLS:(i + 1) * LCOLS, :]
            for later in (1, 2):
                if i + later < 4:
                    at = (i + later) * LCOLS
                    row = jnp.where(lead == later, first[f, at:at + LCOLS, :], row)
            row = jnp.where(i < length, row, 0.0)
            out_ref[f, i * LCOLS:(i + 1) * LCOLS, :] = row.astype(bf16)

    @pl.when(odd == 1)
    def _():
        hand.wait_send()
        out_ref[:, TOK:TOK + 80, :] = jnp.zeros((FRAMES, 80, CH), bf16)

    @pl.when(odd == 0)
    def _():
        hand.wait_recv()
        for f in range(FRAMES):
            got = extra[f].astype(f32)
            place = lax.broadcasted_iota(jnp.int32, (80, CH), 0)
            got = jnp.where(place < (length - 4) * LCOLS, got, 0.0)
            out_ref[f, TOK:TOK + 80, :] = got.astype(bf16)

    to_up.wait_send()
    to_down.wait_send()
    arrived(k_got.at[pl.ds(TOK, TOKENS - TOK)], send_sem.at[0])
    arrived(q_got.at[pl.ds(TOK, TOKENS - TOK)], send_sem.at[1])
    arrived(v_got.at[others], send_sem.at[2])
    arrived(y_got.at[others], send_sem.at[3])


def decode_clip(query, key, value, latent, band_rows, head_weight, conv_in, conv_mid, gamma):
    bf16, f32 = jnp.bfloat16, jnp.float32
    any_space = pl.BlockSpec(memory_space=pltpu.HBM)
    vmem = pl.BlockSpec(memory_space=pltpu.VMEM)
    return pl.pallas_call(
        clip_kernel,
        out_shape=jax.ShapeDtypeStruct((FRAMES, TOK + 80, CH), bf16),
        in_specs=[any_space] * 9,
        out_specs=vmem,
        scratch_shapes=[
            pltpu.VMEM((TOK, HEADS * HEAD), bf16),
            pltpu.VMEM((64, HEADS * HEAD), bf16),
            pltpu.VMEM((SEQ, 80, HEAD), bf16),
            pltpu.VMEM((TOKENS, HEAD), bf16),
            pltpu.VMEM((TOKENS, HEAD), bf16),
            pltpu.VMEM((SEQ, 80, HEAD), bf16),
            pltpu.VMEM((TOKENS, 2 * HEAD), bf16),
            pltpu.VMEM((TOKENS, 2 * HEAD), bf16),
            pltpu.VMEM((TOKENS, HEAD), bf16),
            pltpu.VMEM((TOKENS, HEAD), f32),
            pltpu.VMEM((TOKENS, HEAD), f32),
            pltpu.VMEM((2, QB, KB), f32),
            pltpu.VMEM((2, QB, HEAD), f32),
            pltpu.VMEM((SEQ, 80, HEAD), bf16),
            pltpu.VMEM((SEQ, 80, HEAD), bf16),
            pltpu.SemaphoreType.DMA((10,)),
            pltpu.SemaphoreType.DMA((4,)),
            pltpu.SemaphoreType.DMA((NQ,)),
            pltpu.SemaphoreType.DMA((NK,)),
            pltpu.SemaphoreType.DMA((NK,)),
            pltpu.SemaphoreType.DMA,
            pltpu.VMEM((FRAMES, 4, LCOLS * LAT_CH), bf16),
            pltpu.VMEM((LCOLS * 16, HEAD), f32),
            pltpu.VMEM((9, 48, CH), bf16),
            pltpu.VMEM((8, 80, HEAD), f32),
            pltpu.VMEM((FRAMES * 8, 56, HEAD), f32),
            pltpu.VMEM((4, 48, HEAD), f32),
            pltpu.VMEM((2, 48, HEAD), bf16),
            pltpu.VMEM((2, 48, HEAD), bf16),
            pltpu.VMEM((2, 2, 48, HEAD), bf16),
            pltpu.VMEM((FRAMES, 240, 640), bf16),
            pltpu.VMEM((640, CH), bf16),
            pltpu.VMEM((FRAMES, TOK, CH), f32),
            pltpu.VMEM((FRAMES * 6, 56, CH), f32),
            pltpu.VMEM((FRAMES, TOK, 9 * CH), bf16),
            pltpu.VMEM((FRAMES, 240, HEAD), f32),
            pltpu.VMEM((3, 9 * CH, 256), bf16),
            pltpu.VMEM((9 * CH, 256), bf16),
            pltpu.VMEM((9 * CH, HEAD), bf16),
            pltpu.VMEM((FRAMES, TOK, CH), bf16),
            pltpu.VMEM((FRAMES, 80, CH), bf16),
            pltpu.SemaphoreType.DMA((2,)),
            pltpu.SemaphoreType.DMA((2,)),
            pltpu.SemaphoreType.DMA((2,)),
            pltpu.VMEM((CH,), f32),
            pltpu.SMEM((SEQ,), jnp.int32),
        ],
        compiler_params=pltpu.CompilerParams(
            collective_id=1, has_side_effects=True, vmem_limit_bytes=56 * 2**20
        ),
        cost_estimate=pl.CostEstimate(
            flops=4 * TOKENS * TOKENS * HEAD, bytes_accessed=24 * 2**20,
            transcendentals=TOKENS * TOKENS,
        ),
        name="clip",
    )(
        query, key, value, head_weight.T, latent, conv_in.reshape(9, 48, CH),
        conv_mid.reshape(3, 9 * CH, CH), gamma, band_rows,
    )


def hand_out_kernel(rows_ref, out_ref):
    out_ref[...] = rows_ref[...]


def hand_out(rows):
    frame = pl.BlockSpec((2,) + rows.shape[1:], lambda f: (f, 0, 0))
    return pl.pallas_call(
        hand_out_kernel,
        grid=(2,),
        out_shape=jax.ShapeDtypeStruct(rows.shape, rows.dtype),
        in_specs=[frame],
        out_specs=frame,
        name="hand_out",
    )(rows)


def per_device(query, key, value, latent, band_rows, head_weight, conv_in, conv_mid, gamma):
    rows = decode_clip(
        query, key, value, latent, band_rows, head_weight, conv_in, conv_mid, gamma
    )
    return hand_out(rows).reshape(FRAMES, 3 * BAND, LCOLS, CH)


def solution(mesh):
    return jax.shard_map(
        per_device,
        mesh=mesh,
        in_specs=(
            P(("rep", "seq"), None),
            P(("rep", "seq"), None),
            P(("rep", "seq"), None),
            P("rep", "seq", None),
            P("rep"),
            P(),
            P(),
            P(),
            P(),
        ),
        out_specs=P("rep", "seq", None, None),
        check_vma=False,
    )
```
